32 devices in a mesh: rep: 16 (over z, y, x), tp: 2 (over core).
Axes of the slice: x: 2, y: 2, z: 4, core: 2. Of those that a mesh axis runs over, the one named last changes fastest.
Arguments:
- tokens: bfloat16 [16384, 4096], P('rep', 'tp'), may hold values from -6 to 6
- norm_gain: bfloat16 [4096], P('tp'), may hold values from 0.099609375 to 1.8984375
- local_weights: bfloat16 [65536, 256], P('rep', 'tp'), may hold values from -6 to 6
- anchor: float32 [4096, 256], P('rep', 'tp'), may hold values from -6 to 6
- momentum: float32 [4096, 256], P('rep', 'tp'), may hold values from -3 to 3
- key_grad: bfloat16 [16384, 256], P('rep', 'tp'), may hold values from -6 to 6
Outputs:
- new_keys: bfloat16 [16384, 256], P('rep', 'tp')
- weight_grad: bfloat16 [65536, 256], P('rep', 'tp')
- merged: bfloat16 [65536, 256], P('rep', 'tp')
- new_anchor: float32 [4096, 256], P('rep', 'tp')
- new_momentum: float32 [4096, 256], P('rep', 'tp')
The draws below stay inside these ranges and needn't reach their ends.
All inputs are finite; a program needn't handle non-finite values.
Results may differ from the reference program's by a relative error of at most 0.0058.
Values may be sent and summed in bfloat16 or wider, within the bound.
No kernel may reach another device: no remote copies, remote signals or barrier semaphores. Data moves between devices by JAX's collectives and lax.ppermute only.
A program may use at most 64 MiB of HBM per device.

```python
import math
import jax
import jax.numpy as jnp
from jax import lax

D = 4096
HD = 128
TOK = 1024
KV_WIDTH = 256
N_REP = 16


def level_of(own_key, dims, split, smallest, largest):
    loudness = 1.0
    for position, blocks in split:
        draws = jax.random.uniform(jax.random.fold_in(jax.random.fold_in(own_key, 6), position), (blocks,), jnp.float32, smallest / len(split), largest / len(split))
        loudness = loudness * jnp.repeat(jnp.exp(draws), dims[position] // blocks).reshape((-1,) + (1,) * (len(dims) - 1 - position))
    return loudness


def normal_values(key, dims, scale, limit, shards=(), kind=jnp.bfloat16):
    factor_of = level_of(key, dims, shards, -0.22, 0.18) if shards else 1.0
    array = jax.random.normal(key, dims, jnp.float32) * scale * factor_of
    return jnp.minimum(jnp.maximum(array, -limit), limit).astype(kind)


def setup_inputs(seed: int = 0) -> dict:
    streams_of = jax.random.split(jax.random.key(seed), 7)
    tokens = normal_values(streams_of[0], (TOK * N_REP, D), 1.0, 6.0, ((0, 16), (1, 2)))
    norm_gain = jnp.clip(1.0 + 0.18 * jax.random.normal(streams_of[1], (D,), jnp.float32), 0.099609375, 1.8984375).astype(jnp.bfloat16)
    local_weights = normal_values(streams_of[2], (D * N_REP, KV_WIDTH), 1.0, 6.0, ((0, 16), (1, 2)))
    anchor = normal_values(streams_of[3], (D, KV_WIDTH), 1.0, 6.0, ((0, 16), (1, 2)), jnp.float32)
    momentum = normal_values(streams_of[4], (D, KV_WIDTH), 0.5, 3.0, ((0, 16), (1, 2)), jnp.float32)
    key_grad = normal_values(streams_of[5], (TOK * N_REP, KV_WIDTH), 1.0, 6.0, ((0, 16), (1, 2)))
    return {"tokens": tokens, "norm_gain": norm_gain, "local_weights": local_weights, "anchor": anchor, "momentum": momentum, "key_grad": key_grad}


momentum_rate = 0.9
outer_rate = 0.7
mix_rate = 0.5
rope_base = 500000.0
norm_eps = 1e-05

def angles(row_count):
    positions = jnp.arange(row_count, dtype=jnp.float32)
    freq_table = jnp.exp(-(jnp.arange(HD // 2, dtype=jnp.float32) * 2.0 / HD) * math.log(rope_base))
    turned = positions[:, None] * freq_table[None, :]
    return (jnp.cos(turned), jnp.sin(turned))

def rotate(values, cosine, sine_vals):
    row_count = values.shape[0]
    by_head = values.reshape(row_count, -1, HD)
    lower_half = by_head[..., :HD // 2]
    upper_half = by_head[..., HD // 2:]
    cos_part = cosine[:, None, :]
    sin_part = sine_vals[:, None, :]
    turned = jnp.concatenate([lower_half * cos_part - upper_half * sin_part, upper_half * cos_part + lower_half * sin_part], axis=-1)
    return turned.reshape(row_count, -1)

def normalize(hidden, norm_gain):
    widened = hidden.astype(jnp.float32)
    mean_square = lax.optimization_barrier(jnp.mean(widened * widened, axis=-1, keepdims=True))
    return (widened * lax.rsqrt(mean_square + norm_eps) * norm_gain.astype(jnp.float32)).astype(jnp.bfloat16)

def reference(tokens, norm_gain, local_weights, anchor, momentum, key_grad):
    token_blocks = tokens.reshape(N_REP, TOK, D)
    weight_blocks = local_weights.reshape(N_REP, D, -1)
    grad_blocks = key_grad.reshape(N_REP, TOK, -1)
    cosine, sine_vals = angles(TOK)
    inv_width = 1.0 / math.sqrt(D)

    def replica_step(overall, inputs):
        hidden, weights, grads = inputs
        normed = normalize(hidden, norm_gain)
        raw_keys = jnp.dot(normed, weights, preferred_element_type=jnp.float32) * inv_width
        key_rows = rotate(raw_keys, cosine, sine_vals).astype(jnp.bfloat16)
        raw_grad = rotate(grads.astype(jnp.float32), cosine, -sine_vals).astype(jnp.bfloat16)
        weight_grad = (jnp.dot(normed.T, raw_grad, preferred_element_type=jnp.float32) * inv_width).astype(jnp.bfloat16)
        return (overall + weights.astype(jnp.float32), (key_rows, weight_grad))
    start_sum = jnp.zeros((D, weight_blocks.shape[2]), jnp.float32)
    overall, (key_rows, weight_grad) = lax.scan(replica_step, start_sum, (token_blocks, weight_blocks, grad_blocks))
    mean_weights = overall / N_REP
    change = anchor - mean_weights
    new_momentum = momentum_rate * momentum + change
    new_anchor = anchor - outer_rate * (change + momentum_rate * new_momentum)
    outgoing = new_anchor.astype(jnp.bfloat16).astype(jnp.float32)

    def merge_one(weights):
        widened = weights.astype(jnp.float32)
        return (widened + mix_rate * (outgoing - widened)).astype(jnp.bfloat16)
    merged = lax.map(merge_one, weight_blocks)
    return (key_rows.reshape(N_REP * TOK, -1), weight_grad.reshape(N_REP * D, -1), merged.reshape(N_REP * D, -1), new_anchor, new_momentum)
```

```python
import functools
import math

import jax
import jax.numpy as jnp
from jax import lax
from jax.experimental import pallas as pl
from jax.experimental.pallas import tpu as pltpu
from jax.sharding import PartitionSpec as P

HD = 128


momentum_rate = 0.9
outer_rate = 0.7
mix_rate = 0.5
rope_base = 500000.0
norm_eps = 1e-05


def angles(row_count):
    positions = jnp.arange(row_count, dtype=jnp.float32)
    freq_table = jnp.exp(-(jnp.arange(HD // 2, dtype=jnp.float32) * 2.0 / HD) * math.log(rope_base))
    turned = positions[:, None] * freq_table[None, :]
    return (jnp.cos(turned), jnp.sin(turned))


def rotate(values, cosine, sine_vals):
    lower_half = values[:, : HD // 2]
    upper_half = values[:, HD // 2 :]
    return jnp.concatenate(
        [
            lower_half * cosine - upper_half * sine_vals,
            upper_half * cosine + lower_half * sine_vals,
        ],
        axis=-1,
    )


def swap(value, axis, offset):
    size = lax.axis_size(axis)
    return lax.ppermute(value, axis, [(i, i ^ offset) for i in range(size)])


def key_layer(tokens, norm_gain, local_weights, key_grad):
    cores = lax.axis_size("tp")
    me = lax.axis_index("tp")
    rows, part = tokens.shape
    features = part * cores
    inv_width = 1.0 / math.sqrt(features)
    cosine, sine_vals = angles(rows)

    widened = tokens.astype(jnp.float32)
    squares = jnp.sum(widened * widened, axis=-1)
    blocks = local_weights.reshape(cores, part, HD)
    weights = [lax.dynamic_index_in_dim(blocks, me, 0, keepdims=False)]
    for k in range(1, cores):
        weights.append(swap(lax.dynamic_index_in_dim(blocks, me ^ k, 0, keepdims=False), "tp", k))
    weights = jnp.concatenate(weights, axis=1)

    raw_grad = rotate(key_grad.astype(jnp.float32), cosine, -sine_vals).astype(jnp.bfloat16)
    grads = jnp.concatenate([raw_grad] + [swap(raw_grad, "tp", k) for k in range(1, cores)], axis=1)
    total = squares
    for k in range(1, cores):
        total = total + swap(squares, "tp", k)
    scale = lax.rsqrt(total / features + norm_eps)[:, None]
    normed = (widened * scale * norm_gain.astype(jnp.float32)).astype(jnp.bfloat16)

    partial = jnp.dot(normed, weights, preferred_element_type=jnp.float32)
    raw_keys = partial[:, :HD]
    for k in range(1, cores):
        raw_keys = raw_keys + swap(partial[:, k * HD : (k + 1) * HD], "tp", k)
    key_rows = rotate(raw_keys * inv_width, cosine, sine_vals).astype(jnp.bfloat16)

    contracted = lax.dot_general(
        normed, grads, (((0,), (0,)), ((), ())), preferred_element_type=jnp.float32
    )
    contracted = (contracted * inv_width).astype(jnp.bfloat16)
    weight_grad = jnp.zeros((features, HD), jnp.bfloat16)
    for k in range(cores):
        block = contracted[:, k * HD : (k + 1) * HD]
        if k:
            block = swap(block, "tp", k)
        weight_grad = lax.dynamic_update_slice(weight_grad, block, ((me ^ k) * part, 0))
    return (key_rows, weight_grad)


def merge_kernel(plane, w_ref, *refs):
    *g_refs, out_ref = refs
    me = lax.axis_index("rep")
    far = g_refs[0].shape[0]
    rows = g_refs[0].shape[1]
    for p in range(plane):
        for z in range(far):
            k = p + z * plane
            place = pl.ds(pl.multiple_of((me ^ k) * rows, rows), rows)
            w = w_ref[place, :].astype(jnp.float32)
            g = g_refs[p][z].astype(jnp.float32)
            out_ref[place, :] = (w + mix_rate * (g - w)).astype(jnp.bfloat16)


def merge(local_weights, gathered):
    vmem = pl.BlockSpec(memory_space=pltpu.VMEM)
    return pl.pallas_call(
        functools.partial(merge_kernel, len(gathered)),
        out_shape=jax.ShapeDtypeStruct(local_weights.shape, jnp.bfloat16),
        in_specs=[vmem] * (1 + len(gathered)),
        out_specs=vmem,
        compiler_params=pltpu.CompilerParams(vmem_limit_bytes=32 * 2**20),
    )(local_weights, *gathered)


def outer_step(local_weights, anchor, momentum):
    replicas = lax.axis_size("rep")
    rows = anchor.shape[0]
    chunks = local_weights.reshape(replicas, rows, HD)
    received = lax.all_to_all(chunks, "rep", 0, 0)
    mean_weights = jnp.sum(received.astype(jnp.float32), axis=0) / replicas
    change = anchor - mean_weights
    new_momentum = momentum_rate * momentum + change
    new_anchor = anchor - outer_rate * (change + momentum_rate * new_momentum)
    outgoing = new_anchor.astype(jnp.bfloat16)

    plane = 4
    far = replicas // plane
    column = jnp.stack([outgoing] + [swap(outgoing, "rep", z * plane) for z in range(1, far)])
    gathered = [column] + [swap(column, "rep", p) for p in range(1, plane)]
    merged = merge(local_weights, gathered)
    return (merged, new_anchor, new_momentum)


def body(tokens, norm_gain, local_weights, anchor, momentum, key_grad):
    key_rows, weight_grad = key_layer(tokens, norm_gain, local_weights, key_grad)
    merged, new_anchor, new_momentum = outer_step(local_weights, anchor, momentum)
    return (key_rows, weight_grad, merged, new_anchor, new_momentum)


def solution(mesh):
    split = P("rep", "tp")
    return jax.shard_map(
        body,
        mesh=mesh,
        in_specs=(split, P("tp"), split, split, split, split),
        out_specs=(split,) * 5,
        check_vma=False,
    )
```

```python
import functools
import math

import jax
import jax.numpy as jnp
from jax import lax
from jax.experimental import pallas as pl
from jax.experimental.pallas import tpu as pltpu
from jax.sharding import PartitionSpec as P

HD = 128
PLANE = 4


momentum_rate = 0.9
outer_rate = 0.7
mix_rate = 0.5
rope_base = 500000.0
norm_eps = 1e-05


def angles(row_count):
    positions = jnp.arange(row_count, dtype=jnp.float32)
    freq_table = jnp.exp(-(jnp.arange(HD // 2, dtype=jnp.float32) * 2.0 / HD) * math.log(rope_base))
    turned = positions[:, None] * freq_table[None, :]
    return (jnp.cos(turned), jnp.sin(turned))


def rotate(values, cosine, sine_vals):
    lower_half = values[:, : HD // 2]
    upper_half = values[:, HD // 2 :]
    return jnp.concatenate(
        [
            lower_half * cosine - upper_half * sine_vals,
            upper_half * cosine + lower_half * sine_vals,
        ],
        axis=-1,
    )


def swap(value, axis, offset):
    size = lax.axis_size(axis)
    return lax.ppermute(value, axis, [(i, i ^ offset) for i in range(size)])


def share_weights(local_weights):
    cores = lax.axis_size("tp")
    me = lax.axis_index("tp")
    blocks = local_weights.reshape(cores, -1, HD)
    weights = [lax.dynamic_index_in_dim(blocks, me, 0, keepdims=False)]
    for k in range(1, cores):
        weights.append(swap(lax.dynamic_index_in_dim(blocks, me ^ k, 0, keepdims=False), "tp", k))
    return weights


def normalize(tokens, total, norm_gain):
    features = tokens.shape[1] * lax.axis_size("tp")
    scale = lax.rsqrt(total / features + norm_eps)[:, None]
    return (tokens.astype(jnp.float32) * scale * norm_gain.astype(jnp.float32)).astype(jnp.bfloat16)


def place_blocks(blocks):
    me = lax.axis_index("tp")
    part = blocks[0].shape[0]
    whole = jnp.zeros((len(blocks) * part, HD), blocks[0].dtype)
    for k, block in enumerate(blocks):
        whole = lax.dynamic_update_slice(whole, block, ((me ^ k) * part, 0))
    return whole


def pick_kernel(groups, w_ref, *refs):
    *out_refs, sems = refs
    me = lax.axis_index("rep")
    rows = out_refs[0].shape[1]
    copies = []
    for g, group in enumerate(groups):
        for p in range(PLANE):
            for i, z in enumerate(group):
                place = pl.ds(pl.multiple_of((me ^ (z * PLANE + p)) * rows, rows), rows)
                out = out_refs[g * PLANE + p].at[i]
                copies.append(pltpu.make_async_copy(w_ref.at[place, :], out, sems.at[len(copies)]))
    for copy in copies:
        copy.start()
    for copy in copies:
        copy.wait()


def pick(local_weights, rows, groups):
    shapes = [
        jax.ShapeDtypeStruct((len(group), rows, HD), local_weights.dtype)
        for group in groups
        for _ in range(PLANE)
    ]
    out = pl.pallas_call(
        functools.partial(pick_kernel, groups),
        out_shape=shapes,
        in_specs=[pl.BlockSpec(memory_space=pl.ANY)],
        out_specs=[pl.BlockSpec(memory_space=pltpu.VMEM)] * len(shapes),
        scratch_shapes=[pltpu.SemaphoreType.DMA((PLANE * sum(map(len, groups)),))],
    )(local_weights)
    return [out[g * PLANE : (g + 1) * PLANE] for g in range(len(groups))]


def merge_kernel(order, w_ref, *refs):
    out_ref, w_buf, out_buf, in_sems, out_sems = refs[-5:]
    me = lax.axis_index("rep")
    rows = refs[0].shape[0]
    places = [pl.ds(pl.multiple_of((me ^ k) * rows, rows), rows) for k in order]
    loads = [
        pltpu.make_async_copy(w_ref.at[place, :], w_buf.at[i], in_sems.at[i])
        for i, place in enumerate(places)
    ]
    stores = [
        pltpu.make_async_copy(out_buf.at[i], out_ref.at[place, :], out_sems.at[i])
        for i, place in enumerate(places)
    ]
    for load in loads:
        load.start()
    for i, (load, store) in enumerate(zip(loads, stores)):
        load.wait()
        w = w_buf[i].astype(jnp.float32)
        g = refs[i][...].astype(jnp.float32)
        out_buf[i] = (w + mix_rate * (g - w)).astype(jnp.bfloat16)
        store.start()
    for store in stores:
        store.wait()


def merge(local_weights, chunks, base=None):
    order = tuple(chunks)
    rows = chunks[order[0]].shape[0]
    anywhere = pl.BlockSpec(memory_space=pl.ANY)
    vmem = pl.BlockSpec(memory_space=pltpu.VMEM)
    args = [local_weights, *chunks.values()]
    specs = [anywhere] + [vmem] * len(order)
    aliases = {}
    if base is not None:
        aliases = {len(args): 0}
        args.append(base)
        specs.append(anywhere)
    count = len(order)
    return pl.pallas_call(
        functools.partial(merge_kernel, order),
        out_shape=jax.ShapeDtypeStruct(local_weights.shape, jnp.bfloat16),
        in_specs=specs,
        out_specs=anywhere,
        scratch_shapes=[
            pltpu.VMEM((count, rows, HD), jnp.bfloat16),
            pltpu.VMEM((count, rows, HD), jnp.bfloat16),
            pltpu.SemaphoreType.DMA((count,)),
            pltpu.SemaphoreType.DMA((count,)),
        ],
        input_output_aliases=aliases,
    )(*args)


def after(*values):
    return lax.optimization_barrier(values)


def body(tokens, norm_gain, local_weights, anchor, momentum, key_grad):
    cores = lax.axis_size("tp")
    replicas = lax.axis_size("rep")
    far = replicas // PLANE
    inv_width = 1.0 / math.sqrt(tokens.shape[1] * cores)
    step = max(far // 4, 1)
    zs = list(range(far - 1, -1, -1))
    groups = [zs[:step], zs[step : 2 * step], zs[2 * step :]]

    picked = pick(local_weights, anchor.shape[0], groups)
    picked, tokens, local_weights_tp = after(picked, tokens, local_weights)
    plane = [[swap(group[p], "rep", p) for p in (3, 1, 2)] for group in picked]

    def sum_plane(own, parts):
        total = own.astype(jnp.float32)
        for part in parts:
            total = total + part.astype(jnp.float32)
        return total

    def send_far(group, total):
        return [swap(total[i], "rep", z * PLANE) if z else total[i] for i, z in enumerate(group)]

    weights = share_weights(local_weights_tp)
    widened = tokens.astype(jnp.float32)
    squares = jnp.sum(widened * widened, axis=-1)

    squares, plane[0], key_grad = after(squares, plane[0], key_grad)
    sums = send_far(groups[0], sum_plane(picked[0][0], plane[0]))
    total = squares
    for k in range(1, cores):
        total = total + swap(squares, "tp", k)
    cosine, sine_vals = angles(tokens.shape[0])
    raw_grad = rotate(key_grad.astype(jnp.float32), cosine, -sine_vals).astype(jnp.bfloat16)

    raw_grad, plane[1], total, tokens = after(raw_grad, plane[1], total, tokens)
    sums += send_far(groups[1], sum_plane(picked[1][0], plane[1]))
    grads = jnp.concatenate([raw_grad] + [swap(raw_grad, "tp", k) for k in range(1, cores)], axis=1)
    normed = normalize(tokens, total, norm_gain)
    partial = jnp.dot(normed, jnp.concatenate(weights, axis=1), preferred_element_type=jnp.float32)

    partial, plane[2], tokens, grads = after(partial, plane[2], tokens, grads)
    sums += send_far(groups[2], sum_plane(picked[2][0], plane[2]))
    raw_keys = partial[:, :HD]
    for k in range(1, cores):
        raw_keys = raw_keys + swap(partial[:, k * HD : (k + 1) * HD], "tp", k)
    normed = normalize(tokens, total, norm_gain)
    contracted = lax.dot_general(
        normed, grads, (((0,), (0,)), ((), ())), preferred_element_type=jnp.float32
    )
    contracted = (contracted * inv_width).astype(jnp.bfloat16)

    contracted, sums, raw_keys = after(contracted, sums, raw_keys)
    mean_weights = sum(sums) / replicas
    change = anchor - mean_weights
    new_momentum = momentum_rate * momentum + change
    new_anchor = anchor - outer_rate * (change + momentum_rate * new_momentum)
    outgoing = new_anchor.astype(jnp.bfloat16)

    near = [outgoing] + [swap(outgoing, "rep", p) for p in range(1, PLANE)]
    columns = [swap(outgoing, "rep", z * PLANE) for z in range(1, far)]
    key_rows = rotate(raw_keys * inv_width, cosine, sine_vals).astype(jnp.bfloat16)
    blocks = [contracted[:, :HD]]
    for k in range(1, cores):
        blocks.append(swap(contracted[:, k * HD : (k + 1) * HD], "tp", k))
    weight_grad = place_blocks(blocks)

    gathered = dict(enumerate(near))
    late = {}
    split = far // 4
    for part, start in ((columns[:split], 1), (columns[split:], 1 + split)):
        block = jnp.stack(part)
        late = {}
        for p in range(PLANE):
            moved = swap(block, "rep", p) if p else block
            for i in range(len(part)):
                late[(start + i) * PLANE + p] = moved[i]
        if start == 1:
            gathered.update(late)
    merged = merge(local_weights, gathered)
    merged = merge(local_weights, late, merged)
    return (key_rows, weight_grad, merged, new_anchor, new_momentum)


def solution(mesh):
    split = P("rep", "tp")
    return jax.shard_map(
        body,
        mesh=mesh,
        in_specs=(split, P("tp"), split, split, split, split),
        out_specs=(split,) * 5,
        check_vma=False,
    )
```

```python
import functools
import math

import jax
import jax.numpy as jnp
from jax import lax
from jax.experimental import pallas as pl
from jax.experimental.pallas import tpu as pltpu
from jax.sharding import Mesh, PartitionSpec as P

HD = 128
CUBE = 8
SPAN = 32


momentum_rate = 0.9
outer_rate = 0.7
mix_rate = 0.5
rope_base = 500000.0
norm_eps = 1e-05

VMEM = pl.BlockSpec(memory_space=pltpu.VMEM)
LIGHT = pl.CostEstimate(flops=1, bytes_accessed=1, transcendentals=0)
PARAMS = pltpu.CompilerParams(vmem_limit_bytes=40 * 2**20)


def swap(value, axis, offset):
    size = lax.axis_size(axis)
    if not offset:
        return value
    return lax.ppermute(value, axis, [(i, i ^ offset) for i in range(size)])


def after(*values):
    return lax.optimization_barrier(values)


def rows_at(index, rows):
    return pl.ds(pl.multiple_of(index * rows, rows), rows)


def prepare_kernel(w_ref, grad_ref, cos_ref, sin_ref, *out_refs):
    me = lax.axis_index("tp")
    rows = grad_ref.shape[0]
    part = w_ref.shape[0] // (len(out_refs) + 1)
    lane = lax.broadcasted_iota(jnp.int32, (SPAN, HD), 1)
    lower = lane < HD // 2
    pair = jnp.where(lower, lane, lane - HD // 2).astype(jnp.float32)
    freq = jnp.exp(-(pair * 2.0 / HD) * math.log(rope_base))
    step = lax.broadcasted_iota(jnp.int32, (SPAN, HD), 0).astype(jnp.float32)
    near_cos, near_sin = jnp.cos(step * freq), jnp.sin(step * freq)
    near_sin = jnp.where(lower, -near_sin, near_sin)
    for block in range(0, rows // SPAN, SPAN):
        far = (step + block) * SPAN * freq
        far_cos, far_sin = jnp.cos(far), jnp.sin(far)
        far_sin = jnp.where(lower, -far_sin, far_sin)
        for i in range(min(SPAN, rows // SPAN - block)):
            place = pl.ds((block + i) * SPAN, SPAN)
            a_cos, a_sin = far_cos[i : i + 1], far_sin[i : i + 1]
            cosine = a_cos * near_cos - a_sin * near_sin
            signed = a_sin * near_cos + a_cos * near_sin
            cos_ref[place, :] = cosine
            sin_ref[place, :] = signed
            grad = grad_ref[place, :].astype(jnp.float32)
            turned = grad * cosine - pltpu.roll(grad, HD // 2, 1) * signed
            for out in out_refs:
                out[pl.ds(part + (block + i) * SPAN, SPAN), :] = turned.astype(jnp.bfloat16)
    for k, out in enumerate(out_refs):
        out[:part, :] = w_ref[rows_at(me ^ (k + 1), part), :]


def prepare(local_weights, key_grad):
    cores = lax.axis_size("tp")
    rows = key_grad.shape[0]
    table = jax.ShapeDtypeStruct((rows, HD), jnp.float32)
    packed = jax.ShapeDtypeStruct((local_weights.shape[0] // cores + rows, HD), jnp.bfloat16)
    cosine, signed, *packs = pl.pallas_call(
        prepare_kernel,
        out_shape=[table] * 2 + [packed] * (cores - 1),
        in_specs=[VMEM] * 2,
        out_specs=[VMEM] * (cores + 1),
        compiler_params=PARAMS,
        cost_estimate=LIGHT,
    )(local_weights, key_grad)
    return cosine, signed, packs


def squares_kernel(x_ref, out_ref):
    total = None
    for c in range(x_ref.shape[1] // HD):
        x = x_ref[:, c * HD : (c + 1) * HD].astype(jnp.float32)
        total = x * x if total is None else total + x * x
    out_ref[...] = jnp.sum(total.T, axis=0, keepdims=True)


def squares_of(tokens):
    rows, part = tokens.shape
    block = 256
    out = pl.pallas_call(
        squares_kernel,
        out_shape=jax.ShapeDtypeStruct((1, rows), jnp.float32),
        grid=(rows // block,),
        in_specs=[pl.BlockSpec((block, part), lambda i: (i, 0))],
        out_specs=pl.BlockSpec((1, block), lambda i: (0, i)),
        compiler_params=PARAMS,
        cost_estimate=LIGHT,
    )(tokens)
    return out.reshape(rows)


def turn_kernel(inv_width, own_ref, *refs):
    *other_refs, cos_ref, sin_ref, out_ref = refs
    total = own_ref[:, :HD]
    for other in other_refs:
        total = total + other[...]
    keys = total * inv_width
    turned = keys * cos_ref[...] + pltpu.roll(keys, HD // 2, 1) * sin_ref[...]
    out_ref[...] = turned.astype(jnp.bfloat16)


def turn(inv_width, partial, others, cosine, signed):
    rows = partial.shape[0]
    return pl.pallas_call(
        functools.partial(turn_kernel, inv_width),
        out_shape=jax.ShapeDtypeStruct((rows, HD), jnp.bfloat16),
        in_specs=[VMEM] * (3 + len(others)),
        out_specs=VMEM,
        compiler_params=PARAMS,
        cost_estimate=LIGHT,
    )(partial, *others, cosine, signed)


def normalize(tokens, total, norm_gain):
    features = tokens.shape[1] * lax.axis_size("tp")
    scale = lax.rsqrt(total / features + norm_eps)[:, None]
    return (tokens.astype(jnp.float32) * scale * norm_gain.astype(jnp.float32)).astype(jnp.bfloat16)


def place_kernel(own_ref, *refs):
    *other_refs, out_ref = refs
    me = lax.axis_index("tp")
    part = own_ref.shape[0]
    out_ref[rows_at(me, part), :] = own_ref[:, :HD]
    for k, other in enumerate(other_refs):
        out_ref[rows_at(me ^ (k + 1), part), :] = other[...]


def place_blocks(own, others):
    part = own.shape[0]
    return pl.pallas_call(
        place_kernel,
        out_shape=jax.ShapeDtypeStruct(((1 + len(others)) * part, HD), own.dtype),
        in_specs=[VMEM] * (1 + len(others)),
        out_specs=VMEM,
        compiler_params=PARAMS,
        cost_estimate=LIGHT,
    )(own, *others)


def merge_kernel(w_ref, near_ref, out_ref, out_buf, sems):
    me = lax.axis_index("hi")
    cube, far, rows, _ = near_ref.shape
    stores = []
    for c in range(cube):
        for h in range(far):
            place = rows_at((me ^ h) * cube + c, rows)
            i = len(stores)
            w = w_ref[place, :].astype(jnp.float32)
            g = near_ref[c, h].astype(jnp.float32)
            out_buf[i] = (w + mix_rate * (g - w)).astype(jnp.bfloat16)
            stores.append(pltpu.make_async_copy(out_buf.at[i], out_ref.at[place, :], sems.at[i]))
            stores[-1].start()
    for store in stores:
        store.wait()


def merge(local_weights, near):
    cube, far, rows, _ = near.shape
    return pl.pallas_call(
        merge_kernel,
        out_shape=jax.ShapeDtypeStruct(local_weights.shape, jnp.bfloat16),
        in_specs=[VMEM] * 2,
        out_specs=pl.BlockSpec(memory_space=pl.ANY),
        scratch_shapes=[
            pltpu.VMEM((cube * far, rows, HD), jnp.bfloat16),
            pltpu.SemaphoreType.DMA((cube * far,)),
        ],
        compiler_params=PARAMS,
        cost_estimate=LIGHT,
    )(local_weights, near)


def body(tokens, norm_gain, local_weights, anchor, momentum, key_grad):
    cores = lax.axis_size("tp")
    far = lax.axis_size("hi")
    me = lax.axis_index("hi")
    rows, part = tokens.shape
    own_rows = anchor.shape[0]
    inv_width = 1.0 / math.sqrt(part * cores)

    chunks = local_weights.reshape(far, CUBE, own_rows, HD).transpose(1, 0, 2, 3)
    chunks, tokens, w, key_grad = after(chunks, tokens, local_weights, key_grad)
    received = lax.all_to_all(chunks, "cube", 0, 0)
    squares = squares_of(tokens)
    cosine, signed, packs = prepare(w, key_grad)
    squares_in = [swap(squares, "tp", k) for k in range(1, cores)]
    packs_in = [swap(pack, "tp", k + 1) for k, pack in enumerate(packs)]
    own_weights = lax.dynamic_slice_in_dim(w, lax.axis_index("tp") * part, part, 0)
    weights = jnp.concatenate([own_weights] + [pack[:part] for pack in packs_in], axis=1)
    grads = jnp.concatenate([pack[part:] for pack in [packs[0]] + packs_in], axis=1)
    norm = normalize(tokens, sum(squares_in, squares), norm_gain)
    partial = jnp.dot(norm, weights, preferred_element_type=jnp.float32)

    received, partial, tokens, grads = after(received, partial, tokens, grads)
    summed = jnp.sum(received.astype(jnp.float32), axis=0)
    sums = [
        swap(lax.dynamic_index_in_dim(summed, me ^ h, 0, keepdims=False), "hi", h)
        for h in range(far)
    ]
    keys_in = [swap(partial[:, k * HD : (k + 1) * HD], "tp", k) for k in range(1, cores)]
    norm = normalize(tokens, sum(squares_in, squares), norm_gain)
    contracted = lax.dot_general(
        norm, grads, (((0,), (0,)), ((), ())), preferred_element_type=jnp.float32
    )
    contracted = (contracted * inv_width).astype(jnp.bfloat16)

    contracted, sums, keys_in = after(contracted, sums, keys_in)
    mean_weights = sum(sums) / (far * CUBE)
    change = anchor - mean_weights
    new_momentum = momentum_rate * momentum + change
    new_anchor = anchor - outer_rate * (change + momentum_rate * new_momentum)
    outgoing = new_anchor.astype(jnp.bfloat16)

    column = jnp.stack([swap(outgoing, "hi", h) for h in range(far)])
    grads_in = [swap(contracted[:, k * HD : (k + 1) * HD], "tp", k) for k in range(1, cores)]
    column, grads_in, partial = after(column, grads_in, partial)
    near = lax.all_to_all(jnp.broadcast_to(column, (CUBE, *column.shape)), "cube", 0, 0)
    key_rows = turn(inv_width, partial, keys_in, cosine, signed)
    weight_grad = place_blocks(contracted, grads_in)
    merged = merge(w, near)
    return (key_rows, weight_grad, merged, new_anchor, new_momentum)


def solution(mesh):
    replicas, cores = mesh.devices.shape
    cubes = Mesh(mesh.devices.reshape(replicas // CUBE, CUBE, cores), ("hi", "cube", "tp"))
    split = P(("hi", "cube"), "tp")
    return jax.shard_map(
        body,
        mesh=cubes,
        in_specs=(split, P("tp"), split, split, split, split),
        out_specs=(split,) * 5,
        check_vma=False,
    )
```

```python
import functools
import math

import jax
import jax.numpy as jnp
from jax import lax
from jax.experimental import pallas as pl
from jax.experimental.pallas import tpu as pltpu
from jax.sharding import Mesh, PartitionSpec as P

HD = 128
CUBE = 8
SPAN = 32


momentum_rate = 0.9
outer_rate = 0.7
mix_rate = 0.5
rope_base = 500000.0
norm_eps = 1e-05

VMEM = pl.BlockSpec(memory_space=pltpu.VMEM)
LIGHT = pl.CostEstimate(flops=1, bytes_accessed=1, transcendentals=0)
PARAMS = pltpu.CompilerParams(vmem_limit_bytes=12 * 2**20)


def swap(value, axis, offset):
    size = lax.axis_size(axis)
    if not offset:
        return value
    return lax.ppermute(value, axis, [(i, i ^ offset) for i in range(size)])


def after(*values):
    return lax.optimization_barrier(values)


def rows_at(index, rows):
    return pl.ds(pl.multiple_of(index * rows, rows), rows)


def prepare_kernel(w_ref, grad_ref, cos_ref, sin_ref, *out_refs):
    me = lax.axis_index("tp")
    rows = grad_ref.shape[0]
    part = w_ref.shape[0] // (len(out_refs) + 1)
    lane = lax.broadcasted_iota(jnp.int32, (SPAN, HD), 1)
    lower = lane < HD // 2
    pair = jnp.where(lower, lane, lane - HD // 2).astype(jnp.float32)
    freq = jnp.exp(-(pair * 2.0 / HD) * math.log(rope_base))
    step = lax.broadcasted_iota(jnp.int32, (SPAN, HD), 0).astype(jnp.float32)
    near_cos, near_sin = jnp.cos(step * freq), jnp.sin(step * freq)
    near_sin = jnp.where(lower, -near_sin, near_sin)
    for block in range(0, rows // SPAN, SPAN):
        far = (step + block) * SPAN * freq
        far_cos, far_sin = jnp.cos(far), jnp.sin(far)
        far_sin = jnp.where(lower, -far_sin, far_sin)
        for i in range(min(SPAN, rows // SPAN - block)):
            place = pl.ds((block + i) * SPAN, SPAN)
            a_cos, a_sin = far_cos[i : i + 1], far_sin[i : i + 1]
            cosine = a_cos * near_cos - a_sin * near_sin
            signed = a_sin * near_cos + a_cos * near_sin
            cos_ref[place, :] = cosine
            sin_ref[place, :] = signed
            grad = grad_ref[place, :].astype(jnp.float32)
            turned = grad * cosine - pltpu.roll(grad, HD // 2, 1) * signed
            for out in out_refs:
                out[pl.ds(part + (block + i) * SPAN, SPAN), :] = turned.astype(jnp.bfloat16)
    for k, out in enumerate(out_refs):
        out[:part, :] = w_ref[rows_at(me ^ (k + 1), part), :]


def prepare(local_weights, key_grad):
    cores = lax.axis_size("tp")
    rows = key_grad.shape[0]
    table = jax.ShapeDtypeStruct((rows, HD), jnp.float32)
    packed = jax.ShapeDtypeStruct((local_weights.shape[0] // cores + rows, HD), jnp.bfloat16)
    cosine, signed, *packs = pl.pallas_call(
        prepare_kernel,
        out_shape=[table] * 2 + [packed] * (cores - 1),
        in_specs=[VMEM] * 2,
        out_specs=[VMEM] * (cores + 1),
        compiler_params=PARAMS,
        cost_estimate=LIGHT,
    )(local_weights, key_grad)
    return cosine, signed, packs


def squares_kernel(x_ref, out_ref):
    total = None
    for c in range(x_ref.shape[1] // HD):
        x = x_ref[:, c * HD : (c + 1) * HD].astype(jnp.float32)
        total = x * x if total is None else total + x * x
    out_ref[...] = jnp.sum(total.T, axis=0, keepdims=True)


def squares_of(tokens):
    rows, part = tokens.shape
    block = 256
    out = pl.pallas_call(
        squares_kernel,
        out_shape=jax.ShapeDtypeStruct((1, rows), jnp.float32),
        grid=(rows // block,),
        in_specs=[pl.BlockSpec((block, part), lambda i: (i, 0))],
        out_specs=pl.BlockSpec((1, block), lambda i: (0, i)),
        compiler_params=PARAMS,
        cost_estimate=LIGHT,
    )(tokens)
    return out.reshape(rows)


def turn_kernel(inv_width, own_ref, *refs):
    *other_refs, cos_ref, sin_ref, out_ref = refs
    total = own_ref[:, :HD]
    for other in other_refs:
        total = total + other[...]
    keys = total * inv_width
    turned = keys * cos_ref[...] + pltpu.roll(keys, HD // 2, 1) * sin_ref[...]
    out_ref[...] = turned.astype(jnp.bfloat16)


def turn(inv_width, partial, others, cosine, signed):
    rows = partial.shape[0]
    return pl.pallas_call(
        functools.partial(turn_kernel, inv_width),
        out_shape=jax.ShapeDtypeStruct((rows, HD), jnp.bfloat16),
        in_specs=[VMEM] * (3 + len(others)),
        out_specs=VMEM,
        compiler_params=PARAMS,
        cost_estimate=LIGHT,
    )(partial, *others, cosine, signed)


def normalize(tokens, total, norm_gain):
    features = tokens.shape[1] * lax.axis_size("tp")
    scale = lax.rsqrt(total / features + norm_eps)[:, None]
    return (tokens.astype(jnp.float32) * scale * norm_gain.astype(jnp.float32)).astype(jnp.bfloat16)


def place_kernel(own_ref, *refs):
    *other_refs, out_ref = refs
    me = lax.axis_index("tp")
    part = own_ref.shape[0]
    out_ref[rows_at(me, part), :] = own_ref[:, :HD]
    for k, other in enumerate(other_refs):
        out_ref[rows_at(me ^ (k + 1), part), :] = other[...]


def place_blocks(own, others):
    part = own.shape[0]
    return pl.pallas_call(
        place_kernel,
        out_shape=jax.ShapeDtypeStruct(((1 + len(others)) * part, HD), own.dtype),
        in_specs=[VMEM] * (1 + len(others)),
        out_specs=VMEM,
        compiler_params=PARAMS,
        cost_estimate=LIGHT,
    )(own, *others)


def pick_kernel(order, w_ref, out_ref, sems):
    me = lax.axis_index("hi")
    cube, _, rows, _ = out_ref.shape
    copies = []
    for i, h in enumerate(order):
        for c in range(cube) if len(order) > 1 else [None]:
            if c is None:
                source, target = w_ref.at[rows_at(me ^ h, cube)], out_ref.at[:, 0]
            else:
                source, target = w_ref.at[(me ^ h) * cube + c], out_ref.at[c, i]
            copies.append(pltpu.make_async_copy(source, target, sems.at[len(copies)]))
            copies[-1].start()
    for copy in copies:
        copy.wait()


def pick(chunks, order):
    _, rows, _ = chunks.shape
    return pl.pallas_call(
        functools.partial(pick_kernel, order),
        out_shape=jax.ShapeDtypeStruct((CUBE, len(order), rows, HD), chunks.dtype),
        in_specs=[pl.BlockSpec(memory_space=pl.ANY)],
        out_specs=VMEM,
        scratch_shapes=[pltpu.SemaphoreType.DMA((CUBE * len(order),))],
        compiler_params=PARAMS,
        cost_estimate=LIGHT,
    )(chunks)


def merge_kernel(order, w_ref, near_ref, *refs):
    out_ref, out_buf, sems = refs[-3:]
    me = lax.axis_index("hi")
    cube, _, rows, _ = near_ref.shape
    stores = []
    for c in range(cube):
        for j, h in enumerate(order):
            place = rows_at((me ^ h) * cube + c, rows)
            i = len(stores)
            w = w_ref[place, :].astype(jnp.float32)
            g = near_ref[c, j].astype(jnp.float32)
            out_buf[i] = (w + mix_rate * (g - w)).astype(jnp.bfloat16)
            stores.append(pltpu.make_async_copy(out_buf.at[i], out_ref.at[place, :], sems.at[i]))
            stores[-1].start()
    for store in stores:
        store.wait()


def merge(local_weights, near, order, base=None):
    cube, _, rows, _ = near.shape
    anywhere = pl.BlockSpec(memory_space=pl.ANY)
    return pl.pallas_call(
        functools.partial(merge_kernel, order),
        out_shape=jax.ShapeDtypeStruct(local_weights.shape, jnp.bfloat16),
        in_specs=[VMEM] * 2 + [anywhere] * (base is not None),
        out_specs=anywhere,
        scratch_shapes=[
            pltpu.VMEM((cube * len(order), rows, HD), jnp.bfloat16),
            pltpu.SemaphoreType.DMA((cube * len(order),)),
        ],
        input_output_aliases={} if base is None else {2: 0},
        compiler_params=PARAMS,
        cost_estimate=LIGHT,
    )(local_weights, near, *([] if base is None else [base]))


def body(tokens, norm_gain, local_weights, anchor, momentum, key_grad):
    cores = lax.axis_size("tp")
    far = lax.axis_size("hi")
    rows, part = tokens.shape
    own_rows = anchor.shape[0]
    inv_width = 1.0 / math.sqrt(part * cores)
    others = list(range(1, far))

    chunks = local_weights.reshape(far * CUBE, own_rows, HD)
    sent = pick(chunks, others)
    sent, tokens, w, key_grad, chunks = after(sent, tokens, local_weights, key_grad, chunks)
    received = lax.all_to_all(sent, "cube", 0, 0)
    kept = lax.all_to_all(pick(chunks, [0]), "cube", 0, 0)
    squares = squares_of(tokens)
    squares_in = [swap(squares, "tp", k) for k in range(1, cores)]
    cosine, signed, packs = prepare(w, key_grad)
    packs_in = [swap(pack, "tp", k + 1) for k, pack in enumerate(packs)]

    received, packs_in, tokens, squares_in = after(received, packs_in, tokens, squares_in)
    summed = jnp.sum(received.astype(jnp.float32), axis=0)
    sums = [swap(summed[i], "hi", h) for i, h in enumerate(others)]
    own_weights = lax.dynamic_slice_in_dim(w, lax.axis_index("tp") * part, part, 0)
    weights = jnp.concatenate([own_weights] + [pack[:part] for pack in packs_in], axis=1)
    grads = jnp.concatenate([pack[part:] for pack in [packs[0]] + packs_in], axis=1)
    norm = normalize(tokens, sum(squares_in, squares), norm_gain)
    partial = jnp.dot(norm, weights, preferred_element_type=jnp.float32)
    keys_in = [swap(partial[:, k * HD : (k + 1) * HD], "tp", k) for k in range(1, cores)]

    kept, sums, partial, tokens, grads = after(kept, sums, partial, tokens, grads)
    mean_weights = sum(sums, jnp.sum(kept[:, 0].astype(jnp.float32), axis=0)) / (far * CUBE)
    change = anchor - mean_weights
    new_momentum = momentum_rate * momentum + change
    new_anchor = anchor - outer_rate * (change + momentum_rate * new_momentum)
    outgoing = new_anchor.astype(jnp.bfloat16)

    column = [swap(outgoing, "hi", h) for h in others]
    near = lax.all_to_all(jnp.broadcast_to(outgoing, (CUBE, 1, own_rows, HD)), "cube", 0, 0)
    norm = normalize(tokens, sum(squares_in, squares), norm_gain)
    contracted = lax.dot_general(
        norm, grads, (((0,), (0,)), ((), ())), preferred_element_type=jnp.float32
    )
    contracted = (contracted * inv_width).astype(jnp.bfloat16)

    column, near, contracted, keys_in, partial = after(column, near, contracted, keys_in, partial)
    column = jnp.broadcast_to(jnp.stack(column), (CUBE, len(others), own_rows, HD))
    rest = lax.all_to_all(column, "cube", 0, 0)
    grads_in = [swap(contracted[:, k * HD : (k + 1) * HD], "tp", k) for k in range(1, cores)]
    key_rows = turn(inv_width, partial, keys_in, cosine, signed)
    weight_grad = place_blocks(contracted, grads_in)
    merged = merge(w, near, [0])
    rest, key_rows, weight_grad, merged = after(rest, key_rows, weight_grad, merged)
    merged = merge(w, rest, others, merged)
    return (key_rows, weight_grad, merged, new_anchor, new_momentum)


def solution(mesh):
    replicas, cores = mesh.devices.shape
    cubes = Mesh(mesh.devices.reshape(replicas // CUBE, CUBE, cores), ("hi", "cube", "tp"))
    split = P(("hi", "cube"), "tp")
    return jax.shard_map(
        body,
        mesh=cubes,
        in_specs=(split, P("tp"), split, split, split, split),
        out_specs=(split,) * 5,
        check_vma=False,
    )
```

```python
import functools
import math

import jax
import jax.numpy as jnp
from jax import lax
from jax.experimental import pallas as pl
from jax.experimental.pallas import tpu as pltpu
from jax.sharding import PartitionSpec as P

HD = 128
PLANE = 4
CUBE = 8
SPAN = 32


momentum_rate = 0.9
outer_rate = 0.7
mix_rate = 0.5
rope_base = 500000.0
norm_eps = 1e-05

VMEM = pl.BlockSpec(memory_space=pltpu.VMEM)
LIGHT = pl.CostEstimate(flops=1, bytes_accessed=1, transcendentals=0)
PARAMS = pltpu.CompilerParams(vmem_limit_bytes=12 * 2**20)


def swap(value, axis, offset):
    size = lax.axis_size(axis)
    if not offset:
        return value
    return lax.ppermute(value, axis, [(i, i ^ offset) for i in range(size)])


def after(*values):
    return lax.optimization_barrier(values)


def rows_at(index, rows):
    return pl.ds(pl.multiple_of(index * rows, rows), rows)


def pick_kernel(w_ref, *out_refs):
    me = lax.axis_index("rep")
    far, rows, _ = out_refs[0].shape
    for c, out in enumerate(out_refs):
        for h in range(far):
            out[h] = w_ref[rows_at(me ^ (h * CUBE + c), rows), :]


def pick(local_weights, rows):
    far = local_weights.shape[0] // (CUBE * rows)
    shape = jax.ShapeDtypeStruct((far, rows, HD), local_weights.dtype)
    return pl.pallas_call(
        pick_kernel,
        out_shape=[shape] * CUBE,
        in_specs=[VMEM],
        out_specs=[VMEM] * CUBE,
        compiler_params=PARAMS,
        cost_estimate=LIGHT,
    )(local_weights)


def prepare_kernel(grad_ref, cos_ref, sin_ref, out_ref):
    rows = grad_ref.shape[0]
    lane = lax.broadcasted_iota(jnp.int32, (SPAN, HD), 1)
    lower = lane < HD // 2
    pair = jnp.where(lower, lane, lane - HD // 2).astype(jnp.float32)
    freq = jnp.exp(-(pair * 2.0 / HD) * math.log(rope_base))
    step = lax.broadcasted_iota(jnp.int32, (SPAN, HD), 0).astype(jnp.float32)
    near_cos, near_sin = jnp.cos(step * freq), jnp.sin(step * freq)
    near_sin = jnp.where(lower, -near_sin, near_sin)
    for block in range(0, rows // SPAN, SPAN):
        far = (step + block) * SPAN * freq
        far_cos, far_sin = jnp.cos(far), jnp.sin(far)
        far_sin = jnp.where(lower, -far_sin, far_sin)
        for i in range(min(SPAN, rows // SPAN - block)):
            place = pl.ds((block + i) * SPAN, SPAN)
            a_cos, a_sin = far_cos[i : i + 1], far_sin[i : i + 1]
            cosine = a_cos * near_cos - a_sin * near_sin
            signed = a_sin * near_cos + a_cos * near_sin
            cos_ref[place, :] = cosine
            sin_ref[place, :] = signed
            grad = grad_ref[place, :].astype(jnp.float32)
            turned = grad * cosine - pltpu.roll(grad, HD // 2, 1) * signed
            out_ref[place, :] = turned.astype(jnp.bfloat16)


def prepare(key_grad):
    table = jax.ShapeDtypeStruct(key_grad.shape, jnp.float32)
    return pl.pallas_call(
        prepare_kernel,
        out_shape=[table, table, jax.ShapeDtypeStruct(key_grad.shape, jnp.bfloat16)],
        in_specs=[VMEM],
        out_specs=[VMEM] * 3,
        compiler_params=PARAMS,
        cost_estimate=LIGHT,
    )(key_grad)


def squares_kernel(x_ref, out_ref):
    total = None
    for c in range(x_ref.shape[1] // HD):
        x = x_ref[:, c * HD : (c + 1) * HD].astype(jnp.float32)
        total = x * x if total is None else total + x * x
    out_ref[...] = jnp.sum(total.T, axis=0, keepdims=True)


def squares_of(tokens):
    rows, part = tokens.shape
    block = 256
    out = pl.pallas_call(
        squares_kernel,
        out_shape=jax.ShapeDtypeStruct((1, rows), jnp.float32),
        grid=(rows // block,),
        in_specs=[pl.BlockSpec((block, part), lambda i: (i, 0))],
        out_specs=pl.BlockSpec((1, block), lambda i: (0, i)),
        compiler_params=PARAMS,
        cost_estimate=LIGHT,
    )(tokens)
    return out.reshape(rows)


def turn_kernel(inv_width, raw_ref, cos_ref, sin_ref, out_ref):
    keys = raw_ref[...] * inv_width
    turned = keys * cos_ref[...] + pltpu.roll(keys, HD // 2, 1) * sin_ref[...]
    out_ref[...] = turned.astype(jnp.bfloat16)


def turn(inv_width, raw_keys, cosine, signed):
    return pl.pallas_call(
        functools.partial(turn_kernel, inv_width),
        out_shape=jax.ShapeDtypeStruct(raw_keys.shape, jnp.bfloat16),
        in_specs=[VMEM] * 3,
        out_specs=VMEM,
        compiler_params=PARAMS,
        cost_estimate=LIGHT,
    )(raw_keys, cosine, signed)


def normalize(tokens, scale, norm_gain):
    return (tokens.astype(jnp.float32) * scale * norm_gain.astype(jnp.float32)).astype(jnp.bfloat16)


def place_kernel(*refs):
    *block_refs, out_ref = refs
    me = lax.axis_index("tp")
    part = block_refs[0].shape[0]
    for k, block in enumerate(block_refs):
        out_ref[rows_at(me ^ k, part), :] = block[...]


def place_blocks(blocks):
    part, _ = blocks[0].shape
    return pl.pallas_call(
        place_kernel,
        out_shape=jax.ShapeDtypeStruct((len(blocks) * part, HD), blocks[0].dtype),
        in_specs=[VMEM] * len(blocks),
        out_specs=VMEM,
        compiler_params=PARAMS,
        cost_estimate=LIGHT,
    )(*blocks)


def merge_kernel(offsets, w_ref, *refs):
    count = len(offsets)
    out_ref, out_buf, sems = refs[-3:]
    me = lax.axis_index("rep")
    rows = out_buf.shape[1]
    stores = []
    for chunk, ref in zip(offsets, refs):
        for j, k in enumerate(chunk):
            place = rows_at(me ^ k, rows)
            i = len(stores)
            w = w_ref[place, :].astype(jnp.float32)
            g = ref[j].astype(jnp.float32)
            out_buf[i] = (w + mix_rate * (g - w)).astype(jnp.bfloat16)
            stores.append(pltpu.make_async_copy(out_buf.at[i], out_ref.at[place, :], sems.at[i]))
            stores[-1].start()
    for store in stores:
        store.wait()


def merge(local_weights, chunks, offsets, base=None):
    rows = chunks[0].shape[1]
    anywhere = pl.BlockSpec(memory_space=pl.ANY)
    args = [local_weights, *chunks]
    specs = [VMEM] * len(args)
    aliases = {}
    if base is not None:
        aliases = {len(args): 0}
        args.append(base)
        specs.append(anywhere)
    count = sum(map(len, offsets))
    return pl.pallas_call(
        functools.partial(merge_kernel, offsets),
        out_shape=jax.ShapeDtypeStruct(local_weights.shape, jnp.bfloat16),
        in_specs=specs,
        out_specs=anywhere,
        scratch_shapes=[
            pltpu.VMEM((count, rows, HD), jnp.bfloat16),
            pltpu.SemaphoreType.DMA((count,)),
        ],
        input_output_aliases=aliases,
        compiler_params=PARAMS,
        cost_estimate=LIGHT,
    )(*args)


def body(tokens, norm_gain, local_weights, anchor, momentum, key_grad):
    cores = lax.axis_size("tp")
    replicas = lax.axis_size("rep")
    far = replicas // PLANE
    rows, part = tokens.shape
    inv_width = 1.0 / math.sqrt(part * cores)

    x = [swap(tokens, "tp", k) for k in range(cores)]
    gain = [swap(norm_gain, "tp", k) for k in range(cores)]
    picked = pick(local_weights, anchor.shape[0])
    picked, w, own, key_grad = after(picked, local_weights, tokens, key_grad)
    x[0] = own
    cube = [swap(picked[c], "rep", c) for c in (7, 3, 5, 6, 1, 2, 4)]
    squares = squares_of(own)
    cosine, signed, raw_grad = prepare(key_grad)

    cube, squares, raw_grad, x, gain = after(cube, squares, raw_grad, x, gain)
    total = picked[0].astype(jnp.float32)
    for block in cube:
        total = total + block.astype(jnp.float32)
    sums = [swap(total[h], "rep", h * CUBE) if h else total[h] for h in range(replicas // CUBE)]
    for k in range(1, cores):
        squares = squares + squares_of(x[k])
    scale = lax.rsqrt(squares / (part * cores) + norm_eps)[:, None]
    me = lax.axis_index("tp")
    raw_keys = 0.0
    for k in range(cores):
        block = lax.dynamic_slice_in_dim(w, (me ^ k) * part, part, 0)
        norm = normalize(x[k], scale, gain[k])
        raw_keys = raw_keys + jnp.dot(norm, block, preferred_element_type=jnp.float32)

    sums, raw_keys, x, scale = after(sums, raw_keys, x, scale)
    mean_weights = sum(sums) / replicas
    change = anchor - mean_weights
    new_momentum = momentum_rate * momentum + change
    new_anchor = anchor - outer_rate * (change + momentum_rate * new_momentum)
    outgoing = new_anchor.astype(jnp.bfloat16)[None]

    columns = [swap(outgoing, "rep", z * PLANE) for z in range(far - 1, 0, -1)]
    blocks = []
    for k in range(cores):
        norm = normalize(x[k], scale, gain[k])
        contracted = lax.dot_general(
            norm, raw_grad, (((0,), (0,)), ((), ())), preferred_element_type=jnp.float32
        )
        blocks.append((contracted * inv_width).astype(jnp.bfloat16))
    near = [outgoing] + [swap(outgoing, "rep", p) for p in range(1, PLANE)]
    blocks, near, raw_keys, columns = after(blocks, near, raw_keys, columns)
    block = jnp.concatenate(columns)
    rest = [block] + [swap(block, "rep", p) for p in range(1, PLANE)]
    key_rows = turn(inv_width, raw_keys, cosine, signed)
    weight_grad = place_blocks(blocks)

    zs = range(far - 1, 0, -1)
    early = near + rest[:1]
    merged = merge(w, early, [[p] for p in range(PLANE)] + [[z * PLANE for z in zs]])
    offsets = [[z * PLANE + p for z in zs] for p in range(1, PLANE)]
    key_rows, weight_grad, merged, *rest = after(key_rows, weight_grad, merged, *rest[1:])
    merged = merge(w, rest, offsets, merged)
    return (key_rows, weight_grad, merged, new_anchor, new_momentum)


def solution(mesh):
    split = P("rep", "tp")
    return jax.shard_map(
        body,
        mesh=mesh,
        in_specs=(split, P("tp"), split, split, split, split),
        out_specs=(split,) * 5,
        check_vma=False,
    )
```

```python
import functools
import math

import jax
import jax.numpy as jnp
from jax import lax
from jax.experimental import pallas as pl
from jax.experimental.pallas import tpu as pltpu
from jax.sharding import PartitionSpec as P

HD = 128
PLANE = 4
CUBE = 8
SPAN = 32


momentum_rate = 0.9
outer_rate = 0.7
mix_rate = 0.5
rope_base = 500000.0
norm_eps = 1e-05

VMEM = pl.BlockSpec(memory_space=pltpu.VMEM)
LIGHT = pl.CostEstimate(flops=1, bytes_accessed=1, transcendentals=0)
PARAMS = pltpu.CompilerParams(vmem_limit_bytes=12 * 2**20)


def swap(value, axis, offset):
    size = lax.axis_size(axis)
    if not offset:
        return value
    return lax.ppermute(value, axis, [(i, i ^ offset) for i in range(size)])


def after(*values):
    return lax.optimization_barrier(values)


def rows_at(index, rows):
    return pl.ds(pl.multiple_of(index * rows, rows), rows)


def pick_kernel(cores, w_ref, *out_refs):
    me, core = lax.axis_index("rep"), lax.axis_index("tp")
    far, rows, _ = out_refs[0].shape
    for c in range(CUBE):
        for h in range(far):
            out_refs[c][h] = w_ref[rows_at(me ^ (h * CUBE + c), rows), :]
    for k, out in enumerate(out_refs[CUBE:]):
        out[...] = w_ref[rows_at(core ^ k, out.shape[0]), :]


def pick(local_weights, rows):
    cores = lax.axis_size("tp")
    features = local_weights.shape[0]
    kind = local_weights.dtype
    shapes = [jax.ShapeDtypeStruct((features // (CUBE * rows), rows, HD), kind)] * CUBE
    shapes += [jax.ShapeDtypeStruct((features // cores, HD), kind)] * cores
    out = pl.pallas_call(
        functools.partial(pick_kernel, cores),
        out_shape=shapes,
        in_specs=[VMEM],
        out_specs=[VMEM] * len(shapes),
        compiler_params=PARAMS,
        cost_estimate=LIGHT,
    )(local_weights)
    return out[:CUBE], out[CUBE:]


def prepare_kernel(grad_ref, cos_ref, sin_ref, out_ref):
    rows = grad_ref.shape[0]
    lane = lax.broadcasted_iota(jnp.int32, (SPAN, HD), 1)
    lower = lane < HD // 2
    pair = jnp.where(lower, lane, lane - HD // 2).astype(jnp.float32)
    freq = jnp.exp(-(pair * 2.0 / HD) * math.log(rope_base))
    step = lax.broadcasted_iota(jnp.int32, (SPAN, HD), 0).astype(jnp.float32)
    near_cos, near_sin = jnp.cos(step * freq), jnp.sin(step * freq)
    near_sin = jnp.where(lower, -near_sin, near_sin)
    for block in range(0, rows // SPAN, SPAN):
        far = (step + block) * SPAN * freq
        far_cos, far_sin = jnp.cos(far), jnp.sin(far)
        far_sin = jnp.where(lower, -far_sin, far_sin)
        for i in range(min(SPAN, rows // SPAN - block)):
            place = pl.ds((block + i) * SPAN, SPAN)
            a_cos, a_sin = far_cos[i : i + 1], far_sin[i : i + 1]
            cosine = a_cos * near_cos - a_sin * near_sin
            signed = a_sin * near_cos + a_cos * near_sin
            cos_ref[place, :] = cosine
            sin_ref[place, :] = signed
            grad = grad_ref[place, :].astype(jnp.float32)
            turned = grad * cosine - pltpu.roll(grad, HD // 2, 1) * signed
            out_ref[place, :] = turned.astype(jnp.bfloat16)


def prepare(key_grad):
    table = jax.ShapeDtypeStruct(key_grad.shape, jnp.float32)
    return pl.pallas_call(
        prepare_kernel,
        out_shape=[table, table, jax.ShapeDtypeStruct(key_grad.shape, jnp.bfloat16)],
        in_specs=[VMEM],
        out_specs=[VMEM] * 3,
        compiler_params=PARAMS,
        cost_estimate=LIGHT,
    )(key_grad)


def squares_kernel(x_ref, out_ref):
    total = None
    for c in range(x_ref.shape[1] // HD):
        x = x_ref[:, c * HD : (c + 1) * HD].astype(jnp.float32)
        total = x * x if total is None else total + x * x
    out_ref[...] = jnp.sum(total.T, axis=0, keepdims=True)


def squares_of(tokens):
    rows, part = tokens.shape
    block = 256
    out = pl.pallas_call(
        squares_kernel,
        out_shape=jax.ShapeDtypeStruct((1, rows), jnp.float32),
        grid=(rows // block,),
        in_specs=[pl.BlockSpec((block, part), lambda i: (i, 0))],
        out_specs=pl.BlockSpec((1, block), lambda i: (0, i)),
        compiler_params=PARAMS,
        cost_estimate=LIGHT,
    )(tokens)
    return out.reshape(rows)


def turn_kernel(inv_width, raw_ref, cos_ref, sin_ref, out_ref):
    keys = raw_ref[...] * inv_width
    turned = keys * cos_ref[...] + pltpu.roll(keys, HD // 2, 1) * sin_ref[...]
    out_ref[...] = turned.astype(jnp.bfloat16)


def turn(inv_width, raw_keys, cosine, signed):
    return pl.pallas_call(
        functools.partial(turn_kernel, inv_width),
        out_shape=jax.ShapeDtypeStruct(raw_keys.shape, jnp.bfloat16),
        in_specs=[VMEM] * 3,
        out_specs=VMEM,
        compiler_params=PARAMS,
        cost_estimate=LIGHT,
    )(raw_keys, cosine, signed)


def normalize(tokens, scale, norm_gain):
    return (tokens.astype(jnp.float32) * scale * norm_gain.astype(jnp.float32)).astype(jnp.bfloat16)


def place_kernel(*refs):
    *block_refs, out_ref = refs
    me = lax.axis_index("tp")
    part = block_refs[0].shape[0]
    for k, block in enumerate(block_refs):
        out_ref[rows_at(me ^ k, part), :] = block[...]


def place_blocks(blocks):
    part, _ = blocks[0].shape
    return pl.pallas_call(
        place_kernel,
        out_shape=jax.ShapeDtypeStruct((len(blocks) * part, HD), blocks[0].dtype),
        in_specs=[VMEM] * len(blocks),
        out_specs=VMEM,
        compiler_params=PARAMS,
        cost_estimate=LIGHT,
    )(*blocks)


def merge_kernel(offsets, w_ref, *refs):
    count = len(offsets)
    out_ref, out_buf, sems = refs[-3:]
    me = lax.axis_index("rep")
    rows = out_buf.shape[1]
    stores = []
    for chunk, ref in zip(offsets, refs):
        for j, k in enumerate(chunk):
            place = rows_at(me ^ k, rows)
            i = len(stores)
            w = w_ref[place, :].astype(jnp.float32)
            g = ref[j].astype(jnp.float32)
            out_buf[i] = (w + mix_rate * (g - w)).astype(jnp.bfloat16)
            stores.append(pltpu.make_async_copy(out_buf.at[i], out_ref.at[place, :], sems.at[i]))
            stores[-1].start()
    for store in stores:
        store.wait()


def merge(local_weights, chunks, offsets, base=None):
    rows = chunks[0].shape[1]
    anywhere = pl.BlockSpec(memory_space=pl.ANY)
    args = [local_weights, *chunks]
    specs = [VMEM] * len(args)
    aliases = {}
    if base is not None:
        aliases = {len(args): 0}
        args.append(base)
        specs.append(anywhere)
    count = sum(map(len, offsets))
    return pl.pallas_call(
        functools.partial(merge_kernel, offsets),
        out_shape=jax.ShapeDtypeStruct(local_weights.shape, jnp.bfloat16),
        in_specs=specs,
        out_specs=anywhere,
        scratch_shapes=[
            pltpu.VMEM((count, rows, HD), jnp.bfloat16),
            pltpu.SemaphoreType.DMA((count,)),
        ],
        input_output_aliases=aliases,
        compiler_params=PARAMS,
        cost_estimate=LIGHT,
    )(*args)


def body(tokens, norm_gain, local_weights, anchor, momentum, key_grad):
    cores = lax.axis_size("tp")
    replicas = lax.axis_size("rep")
    far = replicas // PLANE
    rows, part = tokens.shape
    inv_width = 1.0 / math.sqrt(part * cores)

    x = [swap(tokens, "tp", k) for k in range(cores)]
    gain = [swap(norm_gain, "tp", k) for k in range(cores)]
    picked, halves = pick(local_weights, anchor.shape[0])
    picked, halves, w, own, key_grad = after(picked, halves, local_weights, tokens, key_grad)
    x[0] = own
    cube = [swap(picked[c], "rep", c) for c in (1, 2, 4, 7, 3, 5, 6)]
    cosine, signed, raw_grad = prepare(key_grad)
    squares = sum(squares_of(block) for block in x)

    cube, squares, raw_grad, x, gain = after(cube, squares, raw_grad, x, gain)
    total = picked[0].astype(jnp.float32)
    for block in cube:
        total = total + block.astype(jnp.float32)
    sums = [swap(total[h], "rep", h * CUBE) if h else total[h] for h in range(replicas // CUBE)]
    scale = lax.rsqrt(squares / (part * cores) + norm_eps)[:, None]
    raw_keys = 0.0
    for k in range(cores):
        norm = normalize(x[k], scale, gain[k])
        raw_keys = raw_keys + jnp.dot(norm, halves[k], preferred_element_type=jnp.float32)

    def weight_rows(k):
        norm = normalize(x[k], scale, gain[k])
        contracted = lax.dot_general(
            norm, raw_grad, (((0,), (0,)), ((), ())), preferred_element_type=jnp.float32
        )
        return (contracted * inv_width).astype(jnp.bfloat16)

    blocks = [weight_rows(0)]

    sums, raw_keys, blocks, x, scale = after(sums, raw_keys, blocks, x, scale)
    mean_weights = sum(sums) / replicas
    change = anchor - mean_weights
    new_momentum = momentum_rate * momentum + change
    new_anchor = anchor - outer_rate * (change + momentum_rate * new_momentum)
    outgoing = new_anchor.astype(jnp.bfloat16)[None]

    columns = [swap(outgoing, "rep", z * PLANE) for z in range(far - 1, 0, -1)]
    near = [outgoing] + [swap(outgoing, "rep", p) for p in range(1, PLANE)]
    near, raw_keys, x, columns = after(near, raw_keys, x, columns)
    blocks += [weight_rows(k) for k in range(1, cores)]
    block = jnp.concatenate(columns)
    rest = [block] + [swap(block, "rep", p) for p in range(1, PLANE)]
    key_rows = turn(inv_width, raw_keys, cosine, signed)
    weight_grad = place_blocks(blocks)

    zs = range(far - 1, 0, -1)
    early = near + rest[:1]
    merged = merge(w, early, [[p] for p in range(PLANE)] + [[z * PLANE for z in zs]])
    offsets = [[z * PLANE + p for z in zs] for p in range(1, PLANE)]
    key_rows, weight_grad, merged, *rest = after(key_rows, weight_grad, merged, *rest[1:])
    merged = merge(w, rest, offsets, merged)
    return (key_rows, weight_grad, merged, new_anchor, new_momentum)


def solution(mesh):
    split = P("rep", "tp")
    return jax.shard_map(
        body,
        mesh=mesh,
        in_specs=(split, P("tp"), split, split, split, split),
        out_specs=(split,) * 5,
        check_vma=False,
    )
```

```python
import functools
import math

import jax
import jax.numpy as jnp
from jax import lax
from jax.experimental import pallas as pl
from jax.experimental.pallas import tpu as pltpu
from jax.sharding import PartitionSpec as P

HD = 128
PLANE = 4
PAIR = 2 * PLANE
SPAN = 32


momentum_rate = 0.9
outer_rate = 0.7
mix_rate = 0.5
rope_base = 500000.0
norm_eps = 1e-05

VMEM = pl.BlockSpec(memory_space=pltpu.VMEM)
LIGHT = pl.CostEstimate(flops=1, bytes_accessed=1, transcendentals=0)
PARAMS = pltpu.CompilerParams(vmem_limit_bytes=12 * 2**20)


def swap(value, axis, offset):
    size = lax.axis_size(axis)
    if not offset:
        return value
    return lax.ppermute(value, axis, [(i, i ^ offset) for i in range(size)])


def after(*values):
    return lax.optimization_barrier(values)


def rows_at(index, rows):
    return pl.ds(pl.multiple_of(index * rows, rows), rows)


def pick_kernel(groups, w_ref, *out_refs):
    me, core = lax.axis_index("rep"), lax.axis_index("tp")
    rows = out_refs[0].shape[1]
    count = len(groups) * PLANE
    for out, (offsets, p) in zip(out_refs, [(g, p) for g in groups for p in range(PLANE)]):
        for i, k in enumerate(offsets):
            out[i] = w_ref[rows_at(me ^ (k + p), rows), :]
    for k, out in enumerate(out_refs[count:]):
        out[...] = w_ref[rows_at(core ^ k, out.shape[0]), :]


def pick(local_weights, rows, groups):
    cores = lax.axis_size("tp")
    kind = local_weights.dtype
    shapes = [jax.ShapeDtypeStruct((len(g), rows, HD), kind) for g in groups for _ in range(PLANE)]
    shapes += [jax.ShapeDtypeStruct((local_weights.shape[0] // cores, HD), kind)] * cores
    out = pl.pallas_call(
        functools.partial(pick_kernel, groups),
        out_shape=shapes,
        in_specs=[VMEM],
        out_specs=[VMEM] * len(shapes),
        compiler_params=PARAMS,
        cost_estimate=LIGHT,
    )(local_weights)
    count = len(groups) * PLANE
    return [out[i : i + PLANE] for i in range(0, count, PLANE)], out[count:]


def prepare_kernel(grad_ref, cos_ref, sin_ref, out_ref):
    rows = grad_ref.shape[0]
    lane = lax.broadcasted_iota(jnp.int32, (SPAN, HD), 1)
    lower = lane < HD // 2
    pair = jnp.where(lower, lane, lane - HD // 2).astype(jnp.float32)
    freq = jnp.exp(-(pair * 2.0 / HD) * math.log(rope_base))
    step = lax.broadcasted_iota(jnp.int32, (SPAN, HD), 0).astype(jnp.float32)
    near_cos, near_sin = jnp.cos(step * freq), jnp.sin(step * freq)
    near_sin = jnp.where(lower, -near_sin, near_sin)
    for block in range(0, rows // SPAN, SPAN):
        far = (step + block) * SPAN * freq
        far_cos, far_sin = jnp.cos(far), jnp.sin(far)
        far_sin = jnp.where(lower, -far_sin, far_sin)
        for i in range(min(SPAN, rows // SPAN - block)):
            place = pl.ds((block + i) * SPAN, SPAN)
            a_cos, a_sin = far_cos[i : i + 1], far_sin[i : i + 1]
            cosine = a_cos * near_cos - a_sin * near_sin
            signed = a_sin * near_cos + a_cos * near_sin
            cos_ref[place, :] = cosine
            sin_ref[place, :] = signed
            grad = grad_ref[place, :].astype(jnp.float32)
            turned = grad * cosine - pltpu.roll(grad, HD // 2, 1) * signed
            out_ref[place, :] = turned.astype(jnp.bfloat16)


def prepare(key_grad):
    table = jax.ShapeDtypeStruct(key_grad.shape, jnp.float32)
    return pl.pallas_call(
        prepare_kernel,
        out_shape=[table, table, jax.ShapeDtypeStruct(key_grad.shape, jnp.bfloat16)],
        in_specs=[VMEM],
        out_specs=[VMEM] * 3,
        compiler_params=PARAMS,
        cost_estimate=LIGHT,
    )(key_grad)


def squares_kernel(x_ref, out_ref):
    total = None
    for c in range(x_ref.shape[1] // HD):
        x = x_ref[:, c * HD : (c + 1) * HD].astype(jnp.float32)
        total = x * x if total is None else total + x * x
    out_ref[...] = jnp.sum(total.T, axis=0, keepdims=True)


def squares_of(tokens):
    rows, part = tokens.shape
    block = 256
    out = pl.pallas_call(
        squares_kernel,
        out_shape=jax.ShapeDtypeStruct((1, rows), jnp.float32),
        grid=(rows // block,),
        in_specs=[pl.BlockSpec((block, part), lambda i: (i, 0))],
        out_specs=pl.BlockSpec((1, block), lambda i: (0, i)),
        compiler_params=PARAMS,
        cost_estimate=LIGHT,
    )(tokens)
    return out.reshape(rows)


def turn_kernel(inv_width, raw_ref, cos_ref, sin_ref, out_ref):
    keys = raw_ref[...] * inv_width
    turned = keys * cos_ref[...] + pltpu.roll(keys, HD // 2, 1) * sin_ref[...]
    out_ref[...] = turned.astype(jnp.bfloat16)


def turn(inv_width, raw_keys, cosine, signed):
    return pl.pallas_call(
        functools.partial(turn_kernel, inv_width),
        out_shape=jax.ShapeDtypeStruct(raw_keys.shape, jnp.bfloat16),
        in_specs=[VMEM] * 3,
        out_specs=VMEM,
        compiler_params=PARAMS,
        cost_estimate=LIGHT,
    )(raw_keys, cosine, signed)


def normalize(tokens, scale, norm_gain):
    return (tokens.astype(jnp.float32) * scale * norm_gain.astype(jnp.float32)).astype(jnp.bfloat16)


def place_kernel(*refs):
    *block_refs, out_ref = refs
    me = lax.axis_index("tp")
    part = block_refs[0].shape[0]
    for k, block in enumerate(block_refs):
        out_ref[rows_at(me ^ k, part), :] = block[...]


def place_blocks(blocks):
    part, _ = blocks[0].shape
    return pl.pallas_call(
        place_kernel,
        out_shape=jax.ShapeDtypeStruct((len(blocks) * part, HD), blocks[0].dtype),
        in_specs=[VMEM] * len(blocks),
        out_specs=VMEM,
        compiler_params=PARAMS,
        cost_estimate=LIGHT,
    )(*blocks)


def merge_kernel(offsets, w_ref, *refs):
    count = len(offsets)
    out_ref, out_buf, sems = refs[-3:]
    me = lax.axis_index("rep")
    rows = out_buf.shape[1]
    stores = []
    for chunk, ref in zip(offsets, refs):
        for j, k in enumerate(chunk):
            place = rows_at(me ^ k, rows)
            i = len(stores)
            w = w_ref[place, :].astype(jnp.float32)
            g = ref[j].astype(jnp.float32)
            out_buf[i] = (w + mix_rate * (g - w)).astype(jnp.bfloat16)
            stores.append(pltpu.make_async_copy(out_buf.at[i], out_ref.at[place, :], sems.at[i]))
            stores[-1].start()
    for store in stores:
        store.wait()


def merge(local_weights, chunks, offsets, base=None):
    rows = chunks[0].shape[1]
    anywhere = pl.BlockSpec(memory_space=pl.ANY)
    args = [local_weights, *chunks]
    specs = [VMEM] * len(args)
    aliases = {}
    if base is not None:
        aliases = {len(args): 0}
        args.append(base)
        specs.append(anywhere)
    count = sum(map(len, offsets))
    return pl.pallas_call(
        functools.partial(merge_kernel, offsets),
        out_shape=jax.ShapeDtypeStruct(local_weights.shape, jnp.bfloat16),
        in_specs=specs,
        out_specs=anywhere,
        scratch_shapes=[
            pltpu.VMEM((count, rows, HD), jnp.bfloat16),
            pltpu.SemaphoreType.DMA((count,)),
        ],
        input_output_aliases=aliases,
        compiler_params=PARAMS,
        cost_estimate=LIGHT,
    )(*args)


def body(tokens, norm_gain, local_weights, anchor, momentum, key_grad):
    cores = lax.axis_size("tp")
    replicas = lax.axis_size("rep")
    rows, part = tokens.shape
    inv_width = 1.0 / math.sqrt(part * cores)
    far = list(range(PAIR, replicas, PAIR))
    far_side = far + [k + PLANE for k in far]
    near_side = [0, PLANE]
    mates = (1, 2, 3)

    def sum_plane(own, parts):
        total = own.astype(jnp.float32)
        for block in parts:
            total = total + block.astype(jnp.float32)
        return total

    x = [swap(tokens, "tp", k) for k in range(cores)]
    (first, second), halves = pick(local_weights, anchor.shape[0], [far_side, near_side])
    first, second, halves, w, own, key_grad = after(
        first, second, halves, local_weights, tokens, key_grad
    )
    x[0] = own
    first_in = [swap(first[p], "rep", p) for p in mates]
    second_in = [swap(second[p], "rep", p) for p in mates]
    cosine, signed, raw_grad = prepare(key_grad)
    squares = squares_of(own)

    first_in, squares, raw_grad, x, norm_gain = after(first_in, squares, raw_grad, x, norm_gain)
    total = sum_plane(first[0], first_in)
    pair = swap(total[len(far) :], "rep", PLANE)
    for k in range(1, cores):
        squares = squares + squares_of(x[k])

    pair, squares, x, norm_gain = after(pair, squares, x, norm_gain)
    total = total[: len(far)] + pair
    sums = [swap(total[i], "rep", k) for i, k in enumerate(far)]
    gain = [swap(norm_gain, "tp", k) for k in range(cores)]
    scale = lax.rsqrt(squares / (part * cores) + norm_eps)[:, None]

    def key_part(k):
        norm = normalize(x[k], scale, gain[k])
        return jnp.dot(norm, halves[k], preferred_element_type=jnp.float32)

    def weight_rows(k):
        norm = normalize(x[k], scale, gain[k])
        contracted = lax.dot_general(
            norm, raw_grad, (((0,), (0,)), ((), ())), preferred_element_type=jnp.float32
        )
        return (contracted * inv_width).astype(jnp.bfloat16)

    raw_keys = sum(key_part(k) for k in range(cores))

    second_in, raw_keys, x = after(second_in, raw_keys, x)
    total = sum_plane(second[0], second_in)
    sums.append(swap(total[1], "rep", PLANE))

    sums, raw_keys, x, scale, gain = after(sums, raw_keys, x, scale, gain)
    mean_weights = sum(sums, total[0]) / replicas
    change = anchor - mean_weights
    new_momentum = momentum_rate * momentum + change
    new_anchor = anchor - outer_rate * (change + momentum_rate * new_momentum)
    outgoing = new_anchor.astype(jnp.bfloat16)[None]

    mate = swap(outgoing, "rep", PLANE)
    column = [swap(outgoing, "rep", k) for k in far]
    blocks = [weight_rows(0)]
    mate, blocks = after(mate, blocks)
    near = jnp.concatenate([outgoing, mate])
    near = [near] + [swap(near, "rep", p) for p in mates]
    column = jnp.concatenate(column)
    pair = swap(column, "rep", PLANE)
    pair, x, raw_keys = after(pair, x, raw_keys)
    rest = jnp.concatenate([column, pair])
    rest = [rest] + [swap(rest, "rep", p) for p in mates]
    blocks += [weight_rows(k) for k in range(1, cores)]
    key_rows = turn(inv_width, raw_keys, cosine, signed)
    weight_grad = place_blocks(blocks)
    merged = merge(w, near, [[k + p for k in near_side] for p in range(PLANE)])
    key_rows, weight_grad, merged, *rest = after(key_rows, weight_grad, merged, *rest)
    merged = merge(w, rest, [[k + p for k in far_side] for p in range(PLANE)], merged)
    return (key_rows, weight_grad, merged, new_anchor, new_momentum)


def solution(mesh):
    split = P("rep", "tp")
    return jax.shard_map(
        body,
        mesh=mesh,
        in_specs=(split, P("tp"), split, split, split, split),
        out_specs=(split,) * 5,
        check_vma=False,
    )
```

```python
import functools
import math

import jax
import jax.numpy as jnp
from jax import lax
from jax.experimental import pallas as pl
from jax.experimental.pallas import tpu as pltpu
from jax.sharding import PartitionSpec as P

HD = 128
PLANE = 4
PAIR = 2 * PLANE
SPAN = 32


momentum_rate = 0.9
outer_rate = 0.7
mix_rate = 0.5
rope_base = 500000.0
norm_eps = 1e-05

VMEM = pl.BlockSpec(memory_space=pltpu.VMEM)
LIGHT = pl.CostEstimate(flops=1, bytes_accessed=1, transcendentals=0)
PARAMS = pltpu.CompilerParams(vmem_limit_bytes=12 * 2**20)


def swap(value, axis, offset):
    size = lax.axis_size(axis)
    if not offset:
        return value
    return lax.ppermute(value, axis, [(i, i ^ offset) for i in range(size)])


def after(*values):
    return lax.optimization_barrier(values)


def rows_at(index, rows):
    return pl.ds(pl.multiple_of(index * rows, rows), rows)


def pick_kernel(groups, w_ref, *out_refs):
    me, core = lax.axis_index("rep"), lax.axis_index("tp")
    rows = out_refs[0].shape[1]
    count = len(groups) * PLANE
    for out, (offsets, p) in zip(out_refs, [(g, p) for g in groups for p in range(PLANE)]):
        for i, k in enumerate(offsets):
            out[i] = w_ref[rows_at(me ^ (k + p), rows), :]
    for k, out in enumerate(out_refs[count:]):
        out[...] = w_ref[rows_at(core ^ k, out.shape[0]), :]


def pick(local_weights, rows, groups):
    cores = lax.axis_size("tp")
    kind = local_weights.dtype
    shapes = [jax.ShapeDtypeStruct((len(g), rows, HD), kind) for g in groups for _ in range(PLANE)]
    shapes += [jax.ShapeDtypeStruct((local_weights.shape[0] // cores, HD), kind)] * cores
    out = pl.pallas_call(
        functools.partial(pick_kernel, groups),
        out_shape=shapes,
        in_specs=[VMEM],
        out_specs=[VMEM] * len(shapes),
        compiler_params=PARAMS,
        cost_estimate=LIGHT,
    )(local_weights)
    count = len(groups) * PLANE
    return [out[i : i + PLANE] for i in range(0, count, PLANE)], out[count:]


def prepare_kernel(grad_ref, cos_ref, sin_ref, out_ref):
    rows = grad_ref.shape[0]
    lane = lax.broadcasted_iota(jnp.int32, (SPAN, HD), 1)
    lower = lane < HD // 2
    pair = jnp.where(lower, lane, lane - HD // 2).astype(jnp.float32)
    freq = jnp.exp(-(pair * 2.0 / HD) * math.log(rope_base))
    step = lax.broadcasted_iota(jnp.int32, (SPAN, HD), 0).astype(jnp.float32)
    near_cos, near_sin = jnp.cos(step * freq), jnp.sin(step * freq)
    near_sin = jnp.where(lower, -near_sin, near_sin)
    for block in range(0, rows // SPAN, SPAN):
        far = (step + block) * SPAN * freq
        far_cos, far_sin = jnp.cos(far), jnp.sin(far)
        far_sin = jnp.where(lower, -far_sin, far_sin)
        for i in range(min(SPAN, rows // SPAN - block)):
            place = pl.ds((block + i) * SPAN, SPAN)
            a_cos, a_sin = far_cos[i : i + 1], far_sin[i : i + 1]
            cosine = a_cos * near_cos - a_sin * near_sin
            signed = a_sin * near_cos + a_cos * near_sin
            cos_ref[place, :] = cosine
            sin_ref[place, :] = signed
            grad = grad_ref[place, :].astype(jnp.float32)
            turned = grad * cosine - pltpu.roll(grad, HD // 2, 1) * signed
            out_ref[place, :] = turned.astype(jnp.bfloat16)


def prepare(key_grad):
    table = jax.ShapeDtypeStruct(key_grad.shape, jnp.float32)
    return pl.pallas_call(
        prepare_kernel,
        out_shape=[table, table, jax.ShapeDtypeStruct(key_grad.shape, jnp.bfloat16)],
        in_specs=[VMEM],
        out_specs=[VMEM] * 3,
        compiler_params=PARAMS,
        cost_estimate=LIGHT,
    )(key_grad)


def squares_kernel(x_ref, out_ref):
    total = None
    for c in range(x_ref.shape[1] // HD):
        x = x_ref[:, c * HD : (c + 1) * HD].astype(jnp.float32)
        total = x * x if total is None else total + x * x
    out_ref[...] = jnp.sum(total.T, axis=0, keepdims=True)


def squares_of(tokens):
    rows, part = tokens.shape
    block = 256
    out = pl.pallas_call(
        squares_kernel,
        out_shape=jax.ShapeDtypeStruct((1, rows), jnp.float32),
        grid=(rows // block,),
        in_specs=[pl.BlockSpec((block, part), lambda i: (i, 0))],
        out_specs=pl.BlockSpec((1, block), lambda i: (0, i)),
        compiler_params=PARAMS,
        cost_estimate=LIGHT,
    )(tokens)
    return out.reshape(rows)


def turn_kernel(inv_width, raw_ref, cos_ref, sin_ref, out_ref):
    keys = raw_ref[...] * inv_width
    turned = keys * cos_ref[...] + pltpu.roll(keys, HD // 2, 1) * sin_ref[...]
    out_ref[...] = turned.astype(jnp.bfloat16)


def turn(inv_width, raw_keys, cosine, signed):
    return pl.pallas_call(
        functools.partial(turn_kernel, inv_width),
        out_shape=jax.ShapeDtypeStruct(raw_keys.shape, jnp.bfloat16),
        in_specs=[VMEM] * 3,
        out_specs=VMEM,
        compiler_params=PARAMS,
        cost_estimate=LIGHT,
    )(raw_keys, cosine, signed)


def normalize(tokens, scale, norm_gain):
    return (tokens.astype(jnp.float32) * scale * norm_gain.astype(jnp.float32)).astype(jnp.bfloat16)


def place_kernel(*refs):
    *block_refs, out_ref = refs
    me = lax.axis_index("tp")
    part = block_refs[0].shape[0]
    for k, block in enumerate(block_refs):
        out_ref[rows_at(me ^ k, part), :] = block[...]


def place_blocks(blocks):
    part, _ = blocks[0].shape
    return pl.pallas_call(
        place_kernel,
        out_shape=jax.ShapeDtypeStruct((len(blocks) * part, HD), blocks[0].dtype),
        in_specs=[VMEM] * len(blocks),
        out_specs=VMEM,
        compiler_params=PARAMS,
        cost_estimate=LIGHT,
    )(*blocks)


def merge_kernel(offsets, w_ref, *refs):
    count = len(offsets)
    out_ref, out_buf, sems = refs[-3:]
    me = lax.axis_index("rep")
    rows = out_buf.shape[1]
    stores = []
    for chunk, ref in zip(offsets, refs):
        for j, k in enumerate(chunk):
            place = rows_at(me ^ k, rows)
            i = len(stores)
            w = w_ref[place, :].astype(jnp.float32)
            g = ref[j].astype(jnp.float32)
            out_buf[i] = (w + mix_rate * (g - w)).astype(jnp.bfloat16)
            stores.append(pltpu.make_async_copy(out_buf.at[i], out_ref.at[place, :], sems.at[i]))
            stores[-1].start()
    for store in stores:
        store.wait()


def merge(local_weights, chunks, offsets, base=None):
    rows = chunks[0].shape[1]
    anywhere = pl.BlockSpec(memory_space=pl.ANY)
    args = [local_weights, *chunks]
    specs = [VMEM] * len(args)
    aliases = {}
    if base is not None:
        aliases = {len(args): 0}
        args.append(base)
        specs.append(anywhere)
    count = sum(map(len, offsets))
    return pl.pallas_call(
        functools.partial(merge_kernel, offsets),
        out_shape=jax.ShapeDtypeStruct(local_weights.shape, jnp.bfloat16),
        in_specs=specs,
        out_specs=anywhere,
        scratch_shapes=[
            pltpu.VMEM((count, rows, HD), jnp.bfloat16),
            pltpu.SemaphoreType.DMA((count,)),
        ],
        input_output_aliases=aliases,
        compiler_params=PARAMS,
        cost_estimate=LIGHT,
    )(*args)


def body(tokens, norm_gain, local_weights, anchor, momentum, key_grad):
    cores = lax.axis_size("tp")
    replicas = lax.axis_size("rep")
    rows, part = tokens.shape
    inv_width = 1.0 / math.sqrt(part * cores)
    far = list(range(PAIR, replicas, PAIR))
    far_side = far + [k + PLANE for k in far]
    near_side = [0, PLANE]
    mates = (1, 2, 3)

    def sum_plane(own, parts):
        total = own.astype(jnp.float32)
        for block in parts:
            total = total + block.astype(jnp.float32)
        return total

    x = [swap(tokens, "tp", k) for k in range(cores)]
    (first, second), halves = pick(local_weights, anchor.shape[0], [far_side, near_side])
    first, second, halves, w, own, key_grad = after(
        first, second, halves, local_weights, tokens, key_grad
    )
    x[0] = own
    first_in = [swap(first[p], "rep", p) for p in mates]
    second_in = [swap(second[p], "rep", p) for p in mates]
    cosine, signed, raw_grad = prepare(key_grad)
    squares = sum(squares_of(block) for block in x)

    first_in, squares, raw_grad, x, norm_gain = after(first_in, squares, raw_grad, x, norm_gain)
    total = sum_plane(first[0], first_in)
    pair = swap(total[len(far) :], "rep", PLANE)
    pair, squares, x, norm_gain = after(pair, squares, x, norm_gain)
    total = total[: len(far)] + pair
    sums = [swap(total[i], "rep", k) for i, k in enumerate(far)]
    gain = [swap(norm_gain, "tp", k) for k in range(cores)]
    scale = lax.rsqrt(squares / (part * cores) + norm_eps)[:, None]

    def key_part(k):
        norm = normalize(x[k], scale, gain[k])
        return jnp.dot(norm, halves[k], preferred_element_type=jnp.float32)

    def weight_rows(k):
        norm = normalize(x[k], scale, gain[k])
        contracted = lax.dot_general(
            norm, raw_grad, (((0,), (0,)), ((), ())), preferred_element_type=jnp.float32
        )
        return (contracted * inv_width).astype(jnp.bfloat16)

    raw_keys = sum(key_part(k) for k in range(cores))

    second_in, raw_keys, x = after(second_in, raw_keys, x)
    total = sum_plane(second[0], second_in)
    sums.append(swap(total[1], "rep", PLANE))

    key_rows = turn(inv_width, raw_keys, cosine, signed)
    sums, key_rows, x, scale, gain = after(sums, key_rows, x, scale, gain)
    mean_weights = sum(sums, total[0]) / replicas
    change = anchor - mean_weights
    new_momentum = momentum_rate * momentum + change
    new_anchor = anchor - outer_rate * (change + momentum_rate * new_momentum)
    outgoing = new_anchor.astype(jnp.bfloat16)[None]

    mate = swap(outgoing, "rep", PLANE)
    column = [swap(outgoing, "rep", k) for k in far_side]
    near = jnp.concatenate([outgoing, mate])
    near = [near] + [swap(near, "rep", p) for p in mates]
    blocks = [weight_rows(0)]
    column, blocks, x = after(column, blocks, x)
    rest = jnp.concatenate(column)
    rest = [rest] + [swap(rest, "rep", p) for p in mates]
    near, x = after(near, x)
    blocks += [weight_rows(k) for k in range(1, cores)]
    weight_grad = place_blocks(blocks)
    merged = merge(w, near, [[k + p for k in near_side] for p in range(PLANE)])
    key_rows, weight_grad, merged, *rest = after(key_rows, weight_grad, merged, *rest)
    merged = merge(w, rest, [[k + p for k in far_side] for p in range(PLANE)], merged)
    return (key_rows, weight_grad, merged, new_anchor, new_momentum)


def solution(mesh):
    split = P("rep", "tp")
    return jax.shard_map(
        body,
        mesh=mesh,
        in_specs=(split, P("tp"), split, split, split, split),
        out_specs=(split,) * 5,
        check_vma=False,
    )
```

```python
import functools
import math

import jax
import jax.numpy as jnp
from jax import lax
from jax.experimental import pallas as pl
from jax.experimental.pallas import tpu as pltpu
from jax.sharding import PartitionSpec as P

HD = 128
PLANE = 4
PAIR = 2 * PLANE
SPAN = 32


momentum_rate = 0.9
outer_rate = 0.7
mix_rate = 0.5
rope_base = 500000.0
norm_eps = 1e-05

VMEM = pl.BlockSpec(memory_space=pltpu.VMEM)
LIGHT = pl.CostEstimate(flops=1, bytes_accessed=1, transcendentals=0)
PARAMS = pltpu.CompilerParams(vmem_limit_bytes=12 * 2**20)


def swap(value, axis, offset):
    size = lax.axis_size(axis)
    if not offset:
        return value
    return lax.ppermute(value, axis, [(i, i ^ offset) for i in range(size)])


def after(*values):
    return lax.optimization_barrier(values)


def rows_at(index, rows):
    return pl.ds(pl.multiple_of(index * rows, rows), rows)


def pick_kernel(groups, w_ref, *out_refs):
    me, core = lax.axis_index("rep"), lax.axis_index("tp")
    rows = out_refs[0].shape[1]
    count = len(groups) * PLANE
    for out, (offsets, p) in zip(out_refs, [(g, p) for g in groups for p in range(PLANE)]):
        for i, k in enumerate(offsets):
            out[i] = w_ref[rows_at(me ^ (k + p), rows), :]
    for k, out in enumerate(out_refs[count:]):
        out[...] = w_ref[rows_at(core ^ k, out.shape[0]), :]


def pick(local_weights, rows, groups):
    cores = lax.axis_size("tp")
    kind = local_weights.dtype
    shapes = [jax.ShapeDtypeStruct((len(g), rows, HD), kind) for g in groups for _ in range(PLANE)]
    shapes += [jax.ShapeDtypeStruct((local_weights.shape[0] // cores, HD), kind)] * cores
    out = pl.pallas_call(
        functools.partial(pick_kernel, groups),
        out_shape=shapes,
        in_specs=[VMEM],
        out_specs=[VMEM] * len(shapes),
        compiler_params=PARAMS,
        cost_estimate=LIGHT,
    )(local_weights)
    count = len(groups) * PLANE
    return [out[i : i + PLANE] for i in range(0, count, PLANE)], out[count:]


def prepare_kernel(grad_ref, cos_ref, sin_ref, out_ref):
    rows = grad_ref.shape[0]
    lane = lax.broadcasted_iota(jnp.int32, (SPAN, HD), 1)
    lower = lane < HD // 2
    pair = jnp.where(lower, lane, lane - HD // 2).astype(jnp.float32)
    freq = jnp.exp(-(pair * 2.0 / HD) * math.log(rope_base))
    step = lax.broadcasted_iota(jnp.int32, (SPAN, HD), 0).astype(jnp.float32)
    near_cos, near_sin = jnp.cos(step * freq), jnp.sin(step * freq)
    near_sin = jnp.where(lower, -near_sin, near_sin)
    for block in range(0, rows // SPAN, SPAN):
        far = (step + block) * SPAN * freq
        far_cos, far_sin = jnp.cos(far), jnp.sin(far)
        far_sin = jnp.where(lower, -far_sin, far_sin)
        for i in range(min(SPAN, rows // SPAN - block)):
            place = pl.ds((block + i) * SPAN, SPAN)
            a_cos, a_sin = far_cos[i : i + 1], far_sin[i : i + 1]
            cosine = a_cos * near_cos - a_sin * near_sin
            signed = a_sin * near_cos + a_cos * near_sin
            cos_ref[place, :] = cosine
            sin_ref[place, :] = signed
            grad = grad_ref[place, :].astype(jnp.float32)
            turned = grad * cosine - pltpu.roll(grad, HD // 2, 1) * signed
            out_ref[place, :] = turned.astype(jnp.bfloat16)


def prepare(key_grad):
    table = jax.ShapeDtypeStruct(key_grad.shape, jnp.float32)
    return pl.pallas_call(
        prepare_kernel,
        out_shape=[table, table, jax.ShapeDtypeStruct(key_grad.shape, jnp.bfloat16)],
        in_specs=[VMEM],
        out_specs=[VMEM] * 3,
        compiler_params=PARAMS,
        cost_estimate=LIGHT,
    )(key_grad)


def squares_kernel(x_ref, out_ref):
    total = None
    for c in range(x_ref.shape[1] // HD):
        x = x_ref[:, c * HD : (c + 1) * HD].astype(jnp.float32)
        total = x * x if total is None else total + x * x
    out_ref[...] = jnp.sum(total.T, axis=0, keepdims=True)


def squares_of(tokens):
    rows, part = tokens.shape
    block = 256
    out = pl.pallas_call(
        squares_kernel,
        out_shape=jax.ShapeDtypeStruct((1, rows), jnp.float32),
        grid=(rows // block,),
        in_specs=[pl.BlockSpec((block, part), lambda i: (i, 0))],
        out_specs=pl.BlockSpec((1, block), lambda i: (0, i)),
        compiler_params=PARAMS,
        cost_estimate=LIGHT,
    )(tokens)
    return out.reshape(rows)


def turn_kernel(inv_width, raw_ref, cos_ref, sin_ref, out_ref):
    keys = raw_ref[...] * inv_width
    turned = keys * cos_ref[...] + pltpu.roll(keys, HD // 2, 1) * sin_ref[...]
    out_ref[...] = turned.astype(jnp.bfloat16)


def turn(inv_width, raw_keys, cosine, signed):
    return pl.pallas_call(
        functools.partial(turn_kernel, inv_width),
        out_shape=jax.ShapeDtypeStruct(raw_keys.shape, jnp.bfloat16),
        in_specs=[VMEM] * 3,
        out_specs=VMEM,
        compiler_params=PARAMS,
        cost_estimate=LIGHT,
    )(raw_keys, cosine, signed)


def normalize(tokens, scale, norm_gain):
    return (tokens.astype(jnp.float32) * scale * norm_gain.astype(jnp.float32)).astype(jnp.bfloat16)


def place_kernel(*refs):
    *block_refs, out_ref = refs
    me = lax.axis_index("tp")
    part = block_refs[0].shape[0]
    for k, block in enumerate(block_refs):
        out_ref[rows_at(me ^ k, part), :] = block[...]


def place_blocks(blocks):
    part, _ = blocks[0].shape
    return pl.pallas_call(
        place_kernel,
        out_shape=jax.ShapeDtypeStruct((len(blocks) * part, HD), blocks[0].dtype),
        in_specs=[VMEM] * len(blocks),
        out_specs=VMEM,
        compiler_params=PARAMS,
        cost_estimate=LIGHT,
    )(*blocks)


def merge_kernel(offsets, w_ref, *refs):
    count = len(offsets)
    out_ref, out_buf, sems = refs[-3:]
    me = lax.axis_index("rep")
    rows = out_buf.shape[1]
    stores = []
    for chunk, ref in zip(offsets, refs):
        for j, k in enumerate(chunk):
            place = rows_at(me ^ k, rows)
            i = len(stores)
            w = w_ref[place, :].astype(jnp.float32)
            g = ref[j].astype(jnp.float32)
            out_buf[i] = (w + mix_rate * (g - w)).astype(jnp.bfloat16)
            stores.append(pltpu.make_async_copy(out_buf.at[i], out_ref.at[place, :], sems.at[i]))
            stores[-1].start()
    for store in stores:
        store.wait()


def merge(local_weights, chunks, offsets, base=None):
    rows = chunks[0].shape[1]
    anywhere = pl.BlockSpec(memory_space=pl.ANY)
    args = [local_weights, *chunks]
    specs = [VMEM] * len(args)
    aliases = {}
    if base is not None:
        aliases = {len(args): 0}
        args.append(base)
        specs.append(anywhere)
    count = sum(map(len, offsets))
    return pl.pallas_call(
        functools.partial(merge_kernel, offsets),
        out_shape=jax.ShapeDtypeStruct(local_weights.shape, jnp.bfloat16),
        in_specs=specs,
        out_specs=anywhere,
        scratch_shapes=[
            pltpu.VMEM((count, rows, HD), jnp.bfloat16),
            pltpu.SemaphoreType.DMA((count,)),
        ],
        input_output_aliases=aliases,
        compiler_params=PARAMS,
        cost_estimate=LIGHT,
    )(*args)


def body(tokens, norm_gain, local_weights, anchor, momentum, key_grad):
    cores = lax.axis_size("tp")
    replicas = lax.axis_size("rep")
    rows, part = tokens.shape
    inv_width = 1.0 / math.sqrt(part * cores)
    far = list(range(PAIR, replicas, PAIR))
    far_side = far + [k + PLANE for k in far]
    near_side = [0, PLANE]
    mates = (1, 2, 3)

    def sum_plane(own, parts):
        total = own.astype(jnp.float32)
        for block in parts:
            total = total + block.astype(jnp.float32)
        return total

    x = [swap(tokens, "tp", k) for k in range(cores)]
    (first, second), halves = pick(local_weights, anchor.shape[0], [far_side, near_side])
    first, second, halves, w, own, key_grad = after(
        first, second, halves, local_weights, tokens, key_grad
    )
    x[0] = own
    first_in = [swap(first[p], "rep", p) for p in mates]
    second_in = [swap(second[p], "rep", p) for p in mates]
    cosine, signed, raw_grad = prepare(key_grad)
    squares = sum(squares_of(block) for block in x)

    first_in, squares, raw_grad, x, norm_gain = after(first_in, squares, raw_grad, x, norm_gain)
    total = sum_plane(first[0], first_in)
    pair = swap(total[len(far) :], "rep", PLANE)
    pair, squares, x, norm_gain = after(pair, squares, x, norm_gain)
    total = total[: len(far)] + pair
    sums = [swap(total[i], "rep", k) for i, k in enumerate(far)]
    gain = [swap(norm_gain, "tp", k) for k in range(cores)]
    scale = lax.rsqrt(squares / (part * cores) + norm_eps)[:, None]

    def key_part(k):
        norm = normalize(x[k], scale, gain[k])
        return jnp.dot(norm, halves[k], preferred_element_type=jnp.float32)

    def weight_rows(k):
        norm = normalize(x[k], scale, gain[k])
        contracted = lax.dot_general(
            norm, raw_grad, (((0,), (0,)), ((), ())), preferred_element_type=jnp.float32
        )
        return (contracted * inv_width).astype(jnp.bfloat16)

    raw_keys = sum(key_part(k) for k in range(cores))

    second_in, raw_keys, x = after(second_in, raw_keys, x)
    total = sum_plane(second[0], second_in)
    sums.append(swap(total[1], "rep", PLANE))

    key_rows = turn(inv_width, raw_keys, cosine, signed)
    sums[: len(far)], x, scale = after(sums[: len(far)], x, scale)
    blocks = [weight_rows(0)]
    sums, key_rows, blocks, x, scale, gain = after(sums, key_rows, blocks, x, scale, gain)
    mean_weights = sum(sums, total[0]) / replicas
    change = anchor - mean_weights
    new_momentum = momentum_rate * momentum + change
    new_anchor = anchor - outer_rate * (change + momentum_rate * new_momentum)
    outgoing = new_anchor.astype(jnp.bfloat16)[None]

    mate = swap(outgoing, "rep", PLANE)
    column = [swap(outgoing, "rep", k) for k in far_side]
    near = jnp.concatenate([outgoing, mate])
    near = [near] + [swap(near, "rep", p) for p in mates]
    blocks += [weight_rows(k) for k in range(1, cores)]
    weight_grad = place_blocks(blocks)
    column, near, weight_grad = after(column, near, weight_grad)
    rest = jnp.concatenate(column)
    rest = [rest] + [swap(rest, "rep", p) for p in mates]
    merged = merge(w, near, [[k + p for k in near_side] for p in range(PLANE)])
    places = [[k + p for k in far_side] for p in range(PLANE)]
    merged = merge(w, [rest[0], *rest[2:]], [places[0], *places[2:]], merged)
    last, merged = after(rest[1], merged)
    merged = merge(w, [last], places[1:2], merged)
    return (key_rows, weight_grad, merged, new_anchor, new_momentum)


def solution(mesh):
    split = P("rep", "tp")
    return jax.shard_map(
        body,
        mesh=mesh,
        in_specs=(split, P("tp"), split, split, split, split),
        out_specs=(split,) * 5,
        check_vma=False,
    )
```

```python
import functools
import math

import jax
import jax.numpy as jnp
from jax import lax
from jax.experimental import pallas as pl
from jax.experimental.pallas import tpu as pltpu
from jax.sharding import PartitionSpec as P

HD = 128
PLANE = 4
PAIR = 2 * PLANE
SPAN = 32


momentum_rate = 0.9
outer_rate = 0.7
mix_rate = 0.5
rope_base = 500000.0
norm_eps = 1e-05

VMEM = pl.BlockSpec(memory_space=pltpu.VMEM)
LIGHT = pl.CostEstimate(flops=1, bytes_accessed=1, transcendentals=0)
PARAMS = pltpu.CompilerParams(vmem_limit_bytes=12 * 2**20)


def swap(value, axis, offset):
    size = lax.axis_size(axis)
    if not offset:
        return value
    return lax.ppermute(value, axis, [(i, i ^ offset) for i in range(size)])


def after(*values):
    return lax.optimization_barrier(values)


def rows_at(index, rows):
    return pl.ds(pl.multiple_of(index * rows, rows), rows)


def pick_kernel(groups, w_ref, *out_refs):
    me, core = lax.axis_index("rep"), lax.axis_index("tp")
    rows = out_refs[0].shape[1]
    for offsets, out in zip(groups, out_refs):
        for i, k in enumerate(offsets):
            out[i] = w_ref[rows_at(me ^ k, rows), :]
    for k, out in enumerate(out_refs[len(groups) :]):
        out[...] = w_ref[rows_at(core ^ k, out.shape[0]), :]


def pick(local_weights, rows, groups):
    cores = lax.axis_size("tp")
    kind = local_weights.dtype
    shapes = [jax.ShapeDtypeStruct((len(g), rows, HD), kind) for g in groups]
    shapes += [jax.ShapeDtypeStruct((local_weights.shape[0] // cores, HD), kind)] * cores
    out = pl.pallas_call(
        functools.partial(pick_kernel, groups),
        out_shape=shapes,
        in_specs=[VMEM],
        out_specs=[VMEM] * len(shapes),
        compiler_params=PARAMS,
        cost_estimate=LIGHT,
    )(local_weights)
    return out[: len(groups)], out[len(groups) :]


def prepare_kernel(grad_ref, cos_ref, sin_ref, out_ref):
    rows = grad_ref.shape[0]
    lane = lax.broadcasted_iota(jnp.int32, (SPAN, HD), 1)
    lower = lane < HD // 2
    pair = jnp.where(lower, lane, lane - HD // 2).astype(jnp.float32)
    freq = jnp.exp(-(pair * 2.0 / HD) * math.log(rope_base))
    step = lax.broadcasted_iota(jnp.int32, (SPAN, HD), 0).astype(jnp.float32)
    near_cos, near_sin = jnp.cos(step * freq), jnp.sin(step * freq)
    near_sin = jnp.where(lower, -near_sin, near_sin)
    for block in range(0, rows // SPAN, SPAN):
        far = (step + block) * SPAN * freq
        far_cos, far_sin = jnp.cos(far), jnp.sin(far)
        far_sin = jnp.where(lower, -far_sin, far_sin)
        for i in range(min(SPAN, rows // SPAN - block)):
            place = pl.ds((block + i) * SPAN, SPAN)
            a_cos, a_sin = far_cos[i : i + 1], far_sin[i : i + 1]
            cosine = a_cos * near_cos - a_sin * near_sin
            signed = a_sin * near_cos + a_cos * near_sin
            cos_ref[place, :] = cosine
            sin_ref[place, :] = signed
            grad = grad_ref[place, :].astype(jnp.float32)
            turned = grad * cosine - pltpu.roll(grad, HD // 2, 1) * signed
            out_ref[place, :] = turned.astype(jnp.bfloat16)


def prepare(key_grad):
    table = jax.ShapeDtypeStruct(key_grad.shape, jnp.float32)
    return pl.pallas_call(
        prepare_kernel,
        out_shape=[table, table, jax.ShapeDtypeStruct(key_grad.shape, jnp.bfloat16)],
        in_specs=[VMEM],
        out_specs=[VMEM] * 3,
        compiler_params=PARAMS,
        cost_estimate=LIGHT,
    )(key_grad)


def squares_kernel(x_ref, out_ref):
    total = None
    for c in range(x_ref.shape[1] // HD):
        x = x_ref[:, c * HD : (c + 1) * HD].astype(jnp.float32)
        total = x * x if total is None else total + x * x
    out_ref[...] = jnp.sum(total.T, axis=0, keepdims=True)


def squares_of(tokens):
    rows, part = tokens.shape
    block = 256
    out = pl.pallas_call(
        squares_kernel,
        out_shape=jax.ShapeDtypeStruct((1, rows), jnp.float32),
        grid=(rows // block,),
        in_specs=[pl.BlockSpec((block, part), lambda i: (i, 0))],
        out_specs=pl.BlockSpec((1, block), lambda i: (0, i)),
        compiler_params=PARAMS,
        cost_estimate=LIGHT,
    )(tokens)
    return out.reshape(rows)


def turn_kernel(inv_width, raw_ref, cos_ref, sin_ref, out_ref):
    keys = raw_ref[...] * inv_width
    turned = keys * cos_ref[...] + pltpu.roll(keys, HD // 2, 1) * sin_ref[...]
    out_ref[...] = turned.astype(jnp.bfloat16)


def turn(inv_width, raw_keys, cosine, signed):
    return pl.pallas_call(
        functools.partial(turn_kernel, inv_width),
        out_shape=jax.ShapeDtypeStruct(raw_keys.shape, jnp.bfloat16),
        in_specs=[VMEM] * 3,
        out_specs=VMEM,
        compiler_params=PARAMS,
        cost_estimate=LIGHT,
    )(raw_keys, cosine, signed)


def normalize(tokens, scale, norm_gain):
    return (tokens.astype(jnp.float32) * scale * norm_gain.astype(jnp.float32)).astype(jnp.bfloat16)


def place_kernel(*refs):
    *block_refs, out_ref = refs
    me = lax.axis_index("tp")
    part = block_refs[0].shape[0]
    for k, block in enumerate(block_refs):
        out_ref[rows_at(me ^ k, part), :] = block[...]


def place_blocks(blocks):
    part, _ = blocks[0].shape
    return pl.pallas_call(
        place_kernel,
        out_shape=jax.ShapeDtypeStruct((len(blocks) * part, HD), blocks[0].dtype),
        in_specs=[VMEM] * len(blocks),
        out_specs=VMEM,
        compiler_params=PARAMS,
        cost_estimate=LIGHT,
    )(*blocks)


def merge_kernel(offsets, w_ref, *refs):
    count = len(offsets)
    out_ref, out_buf, sems = refs[-3:]
    me = lax.axis_index("rep")
    rows = out_buf.shape[1]
    stores = []
    for chunk, ref in zip(offsets, refs):
        for j, k in enumerate(chunk):
            place = rows_at(me ^ k, rows)
            i = len(stores)
            w = w_ref[place, :].astype(jnp.float32)
            g = ref[j].astype(jnp.float32)
            out_buf[i] = (w + mix_rate * (g - w)).astype(jnp.bfloat16)
            stores.append(pltpu.make_async_copy(out_buf.at[i], out_ref.at[place, :], sems.at[i]))
            stores[-1].start()
    for store in stores:
        store.wait()


def merge(local_weights, chunks, offsets, base=None):
    rows = chunks[0].shape[1]
    anywhere = pl.BlockSpec(memory_space=pl.ANY)
    args = [local_weights, *chunks]
    specs = [VMEM] * len(args)
    aliases = {}
    if base is not None:
        aliases = {len(args): 0}
        args.append(base)
        specs.append(anywhere)
    count = sum(map(len, offsets))
    return pl.pallas_call(
        functools.partial(merge_kernel, offsets),
        out_shape=jax.ShapeDtypeStruct(local_weights.shape, jnp.bfloat16),
        in_specs=specs,
        out_specs=anywhere,
        scratch_shapes=[
            pltpu.VMEM((count, rows, HD), jnp.bfloat16),
            pltpu.SemaphoreType.DMA((count,)),
        ],
        input_output_aliases=aliases,
        compiler_params=PARAMS,
        cost_estimate=LIGHT,
    )(*args)


def body(tokens, norm_gain, local_weights, anchor, momentum, key_grad):
    cores = lax.axis_size("tp")
    replicas = lax.axis_size("rep")
    rows, part = tokens.shape
    inv_width = 1.0 / math.sqrt(part * cores)
    far = list(range(PAIR, replicas, PAIR))
    far_side = far + [k + PLANE for k in far]
    near_side = [0, PLANE]

    mates = (1, 2, 3)

    def sum_plane(own, parts):
        total = own.astype(jnp.float32)
        for block in parts:
            total = total + block.astype(jnp.float32)
        return total

    def shifted(side, *steps):
        return [k + step for step in steps for k in side]

    x = [swap(tokens, "tp", k) for k in range(cores)]
    groups = [shifted(side, p) for side in (far_side, near_side) for p in range(PLANE)]
    picked, halves = pick(local_weights, anchor.shape[0], groups)
    picked, halves, w, own, key_grad = after(picked, halves, local_weights, tokens, key_grad)
    first, second = picked[:PLANE], picked[PLANE:]
    x[0] = own
    first_in = [swap(first[p], "rep", p) for p in mates]
    second_in = [swap(second[p], "rep", p) for p in mates]
    cosine, signed, raw_grad = prepare(key_grad)
    squares = sum(squares_of(block) for block in x)

    first_in, squares, raw_grad, x, norm_gain = after(first_in, squares, raw_grad, x, norm_gain)
    total = sum_plane(first[0], first_in)
    pair = swap(total[len(far) :], "rep", PLANE)
    pair, squares, x, norm_gain = after(pair, squares, x, norm_gain)
    total = total[: len(far)] + pair
    sums = [swap(total[i], "rep", k) for i, k in enumerate(far)]
    gain = [swap(norm_gain, "tp", k) for k in range(cores)]
    scale = lax.rsqrt(squares / (part * cores) + norm_eps)[:, None]

    def key_part(k):
        norm = normalize(x[k], scale, gain[k])
        return jnp.dot(norm, halves[k], preferred_element_type=jnp.float32)

    def weight_rows(k):
        norm = normalize(x[k], scale, gain[k])
        contracted = lax.dot_general(
            norm, raw_grad, (((0,), (0,)), ((), ())), preferred_element_type=jnp.float32
        )
        return (contracted * inv_width).astype(jnp.bfloat16)

    raw_keys = sum(key_part(k) for k in range(cores))

    second_in, raw_keys, x = after(second_in, raw_keys, x)
    total = sum_plane(second[0], second_in)
    sums.append(swap(total[1], "rep", PLANE))

    key_rows = turn(inv_width, raw_keys, cosine, signed)
    sums[: len(far)], x, scale = after(sums[: len(far)], x, scale)
    blocks = [weight_rows(0)]
    sums, key_rows, blocks, x, scale, gain = after(sums, key_rows, blocks, x, scale, gain)
    mean_weights = sum(sums, total[0]) / replicas
    change = anchor - mean_weights
    new_momentum = momentum_rate * momentum + change
    new_anchor = anchor - outer_rate * (change + momentum_rate * new_momentum)
    outgoing = new_anchor.astype(jnp.bfloat16)[None]

    mate = swap(outgoing, "rep", PLANE)
    column = [swap(outgoing, "rep", k) for k in far_side]
    near = jnp.concatenate([outgoing, mate])
    near_in = swap(near, "rep", 2)
    column = jnp.concatenate(column)
    near, near_in, column = after(near, near_in, column)
    column_in = swap(column, "rep", 1)
    near = jnp.concatenate([near, near_in])
    near_in = swap(near, "rep", 1)
    column, column_in, x = after(column, column_in, x)
    column = jnp.concatenate([column, column_in])
    column_in = swap(column, "rep", 2)
    blocks += [weight_rows(k) for k in range(1, cores)]
    weight_grad = place_blocks(blocks)
    here = [shifted(near_side, 0, 2), shifted(far_side, 0, 1)]
    merged = merge(w, [near, column], here)
    weight_grad, merged, column_in = after(weight_grad, merged, column_in)
    merged = merge(w, [column_in], [shifted(far_side, 2, 3)], merged)
    near_in, merged = after(near_in, merged)
    merged = merge(w, [near_in], [shifted(near_side, 1, 3)], merged)
    return (key_rows, weight_grad, merged, new_anchor, new_momentum)


def solution(mesh):
    split = P("rep", "tp")
    return jax.shard_map(
        body,
        mesh=mesh,
        in_specs=(split, P("tp"), split, split, split, split),
        out_specs=(split,) * 5,
        check_vma=False,
    )
```

```python
import functools
import math

import jax
import jax.numpy as jnp
from jax import lax
from jax.experimental import pallas as pl
from jax.experimental.pallas import tpu as pltpu
from jax.sharding import PartitionSpec as P

HD = 128
PLANE = 4
PAIR = 2 * PLANE
SPAN = 32


momentum_rate = 0.9
outer_rate = 0.7
mix_rate = 0.5
rope_base = 500000.0
norm_eps = 1e-05

VMEM = pl.BlockSpec(memory_space=pltpu.VMEM)
LIGHT = pl.CostEstimate(flops=1, bytes_accessed=1, transcendentals=0)
PARAMS = pltpu.CompilerParams(vmem_limit_bytes=12 * 2**20)


def swap(value, axis, offset):
    size = lax.axis_size(axis)
    if not offset:
        return value
    return lax.ppermute(value, axis, [(i, i ^ offset) for i in range(size)])


def after(*values):
    return lax.optimization_barrier(values)


def rows_at(index, rows):
    return pl.ds(pl.multiple_of(index * rows, rows), rows)


def pick_kernel(groups, w_ref, *out_refs):
    me, core = lax.axis_index("rep"), lax.axis_index("tp")
    rows = out_refs[0].shape[1]
    count = len(groups) * PLANE
    for out, (offsets, p) in zip(out_refs, [(g, p) for g in groups for p in range(PLANE)]):
        for i, k in enumerate(offsets):
            out[i] = w_ref[rows_at(me ^ (k + p), rows), :]
    for k, out in enumerate(out_refs[count:]):
        out[...] = w_ref[rows_at(core ^ k, out.shape[0]), :]


def pick(local_weights, rows, groups):
    cores = lax.axis_size("tp")
    kind = local_weights.dtype
    shapes = [jax.ShapeDtypeStruct((len(g), rows, HD), kind) for g in groups for _ in range(PLANE)]
    shapes += [jax.ShapeDtypeStruct((local_weights.shape[0] // cores, HD), kind)] * cores
    out = pl.pallas_call(
        functools.partial(pick_kernel, groups),
        out_shape=shapes,
        in_specs=[VMEM],
        out_specs=[VMEM] * len(shapes),
        compiler_params=PARAMS,
        cost_estimate=LIGHT,
    )(local_weights)
    count = len(groups) * PLANE
    return [out[i : i + PLANE] for i in range(0, count, PLANE)], out[count:]


def prepare_kernel(grad_ref, cos_ref, sin_ref, out_ref):
    rows = grad_ref.shape[0]
    lane = lax.broadcasted_iota(jnp.int32, (SPAN, HD), 1)
    lower = lane < HD // 2
    pair = jnp.where(lower, lane, lane - HD // 2).astype(jnp.float32)
    freq = jnp.exp(-(pair * 2.0 / HD) * math.log(rope_base))
    step = lax.broadcasted_iota(jnp.int32, (SPAN, HD), 0).astype(jnp.float32)
    near_cos, near_sin = jnp.cos(step * freq), jnp.sin(step * freq)
    near_sin = jnp.where(lower, -near_sin, near_sin)
    for block in range(0, rows // SPAN, SPAN):
        far = (step + block) * SPAN * freq
        far_cos, far_sin = jnp.cos(far), jnp.sin(far)
        far_sin = jnp.where(lower, -far_sin, far_sin)
        for i in range(min(SPAN, rows // SPAN - block)):
            place = pl.ds((block + i) * SPAN, SPAN)
            a_cos, a_sin = far_cos[i : i + 1], far_sin[i : i + 1]
            cosine = a_cos * near_cos - a_sin * near_sin
            signed = a_sin * near_cos + a_cos * near_sin
            cos_ref[place, :] = cosine
            sin_ref[place, :] = signed
            grad = grad_ref[place, :].astype(jnp.float32)
            turned = grad * cosine - pltpu.roll(grad, HD // 2, 1) * signed
            out_ref[place, :] = turned.astype(jnp.bfloat16)


def prepare(key_grad):
    table = jax.ShapeDtypeStruct(key_grad.shape, jnp.float32)
    return pl.pallas_call(
        prepare_kernel,
        out_shape=[table, table, jax.ShapeDtypeStruct(key_grad.shape, jnp.bfloat16)],
        in_specs=[VMEM],
        out_specs=[VMEM] * 3,
        compiler_params=PARAMS,
        cost_estimate=LIGHT,
    )(key_grad)


def squares_kernel(x_ref, out_ref):
    total = None
    for c in range(x_ref.shape[1] // HD):
        x = x_ref[:, c * HD : (c + 1) * HD].astype(jnp.float32)
        total = x * x if total is None else total + x * x
    out_ref[...] = jnp.sum(total.T, axis=0, keepdims=True)


def squares_of(tokens):
    rows, part = tokens.shape
    block = 256
    out = pl.pallas_call(
        squares_kernel,
        out_shape=jax.ShapeDtypeStruct((1, rows), jnp.float32),
        grid=(rows // block,),
        in_specs=[pl.BlockSpec((block, part), lambda i: (i, 0))],
        out_specs=pl.BlockSpec((1, block), lambda i: (0, i)),
        compiler_params=PARAMS,
        cost_estimate=LIGHT,
    )(tokens)
    return out.reshape(rows)


def turn_kernel(inv_width, raw_ref, cos_ref, sin_ref, out_ref):
    keys = raw_ref[...] * inv_width
    turned = keys * cos_ref[...] + pltpu.roll(keys, HD // 2, 1) * sin_ref[...]
    out_ref[...] = turned.astype(jnp.bfloat16)


def turn(inv_width, raw_keys, cosine, signed):
    return pl.pallas_call(
        functools.partial(turn_kernel, inv_width),
        out_shape=jax.ShapeDtypeStruct(raw_keys.shape, jnp.bfloat16),
        in_specs=[VMEM] * 3,
        out_specs=VMEM,
        compiler_params=PARAMS,
        cost_estimate=LIGHT,
    )(raw_keys, cosine, signed)


def normalize(tokens, scale, norm_gain):
    return (tokens.astype(jnp.float32) * scale * norm_gain.astype(jnp.float32)).astype(jnp.bfloat16)


def place_kernel(*refs):
    *block_refs, out_ref = refs
    me = lax.axis_index("tp")
    part = block_refs[0].shape[0]
    for k, block in enumerate(block_refs):
        out_ref[rows_at(me ^ k, part), :] = block[...]


def place_blocks(blocks):
    part, _ = blocks[0].shape
    return pl.pallas_call(
        place_kernel,
        out_shape=jax.ShapeDtypeStruct((len(blocks) * part, HD), blocks[0].dtype),
        in_specs=[VMEM] * len(blocks),
        out_specs=VMEM,
        compiler_params=PARAMS,
        cost_estimate=LIGHT,
    )(*blocks)


def merge_kernel(offsets, w_ref, *refs):
    count = len(offsets)
    out_ref, out_buf, sems = refs[-3:]
    me = lax.axis_index("rep")
    rows = out_buf.shape[1]
    stores = []
    for chunk, ref in zip(offsets, refs):
        for j, k in enumerate(chunk):
            place = rows_at(me ^ k, rows)
            i = len(stores)
            w = w_ref[place, :].astype(jnp.float32)
            g = ref[j].astype(jnp.float32)
            out_buf[i] = (w + mix_rate * (g - w)).astype(jnp.bfloat16)
            stores.append(pltpu.make_async_copy(out_buf.at[i], out_ref.at[place, :], sems.at[i]))
            stores[-1].start()
    for store in stores:
        store.wait()


def merge(local_weights, chunks, offsets, base=None):
    rows = chunks[0].shape[1]
    anywhere = pl.BlockSpec(memory_space=pl.ANY)
    args = [local_weights, *chunks]
    specs = [VMEM] * len(args)
    aliases = {}
    if base is not None:
        aliases = {len(args): 0}
        args.append(base)
        specs.append(anywhere)
    count = sum(map(len, offsets))
    return pl.pallas_call(
        functools.partial(merge_kernel, offsets),
        out_shape=jax.ShapeDtypeStruct(local_weights.shape, jnp.bfloat16),
        in_specs=specs,
        out_specs=anywhere,
        scratch_shapes=[
            pltpu.VMEM((count, rows, HD), jnp.bfloat16),
            pltpu.SemaphoreType.DMA((count,)),
        ],
        input_output_aliases=aliases,
        compiler_params=PARAMS,
        cost_estimate=LIGHT,
    )(*args)


def body(tokens, norm_gain, local_weights, anchor, momentum, key_grad):
    cores = lax.axis_size("tp")
    replicas = lax.axis_size("rep")
    rows, part = tokens.shape
    inv_width = 1.0 / math.sqrt(part * cores)
    far = list(range(PAIR, replicas, PAIR))
    far_side = far + [k + PLANE for k in far]
    near_side = [0, PLANE]
    mates = (1, 2, 3)

    def sum_plane(own, parts):
        total = own.astype(jnp.float32)
        for block in parts:
            total = total + block.astype(jnp.float32)
        return total

    x = [swap(tokens, "tp", k) for k in range(cores)]
    (first, second), halves = pick(local_weights, anchor.shape[0], [far_side, near_side])
    first, second, halves, w, own, key_grad = after(
        first, second, halves, local_weights, tokens, key_grad
    )
    x[0] = own
    first_in = [swap(first[p], "rep", p) for p in mates]
    second_in = [swap(second[p], "rep", p) for p in mates]
    cosine, signed, raw_grad = prepare(key_grad)
    squares = sum(squares_of(block) for block in x)

    first_in, squares, raw_grad, x, norm_gain = after(first_in, squares, raw_grad, x, norm_gain)
    total = sum_plane(first[0], first_in)
    pair = swap(total[len(far) :], "rep", PLANE)
    pair, squares, x, norm_gain = after(pair, squares, x, norm_gain)
    total = total[: len(far)] + pair
    sums = [swap(total[i], "rep", k) for i, k in enumerate(far)]
    gain = [swap(norm_gain, "tp", k) for k in range(cores)]
    scale = lax.rsqrt(squares / (part * cores) + norm_eps)[:, None]

    def key_part(k):
        norm = normalize(x[k], scale, gain[k])
        return jnp.dot(norm, halves[k], preferred_element_type=jnp.float32)

    def weight_rows(k):
        norm = normalize(x[k], scale, gain[k])
        contracted = lax.dot_general(
            norm, raw_grad, (((0,), (0,)), ((), ())), preferred_element_type=jnp.float32
        )
        return (contracted * inv_width).astype(jnp.bfloat16)

    raw_keys = sum(key_part(k) for k in range(cores))

    second_in, raw_keys, x = after(second_in, raw_keys, x)
    total = sum_plane(second[0], second_in)
    sums.append(swap(total[1], "rep", PLANE))

    key_rows = turn(inv_width, raw_keys, cosine, signed)
    sums[: len(far)], x, scale = after(sums[: len(far)], x, scale)
    blocks = [weight_rows(0)]
    sums, key_rows, blocks, x, scale, gain = after(sums, key_rows, blocks, x, scale, gain)
    mean_weights = sum(sums, total[0]) / replicas
    change = anchor - mean_weights
    new_momentum = momentum_rate * momentum + change
    new_anchor = anchor - outer_rate * (change + momentum_rate * new_momentum)
    outgoing = new_anchor.astype(jnp.bfloat16)[None]

    mate = swap(outgoing, "rep", PLANE)
    column = [swap(outgoing, "rep", k) for k in far_side]
    mate, x = after(mate, x)
    near = jnp.concatenate([outgoing, mate])
    near = [near] + [swap(near, "rep", p) for p in mates]
    blocks += [weight_rows(k) for k in range(1, cores)]
    column, blocks = after(column, blocks)
    rest = jnp.concatenate(column)
    rest = [rest] + [swap(rest, "rep", p) for p in mates]
    weight_grad = place_blocks(blocks)
    near, weight_grad = after(near, weight_grad)
    merged = merge(w, near, [[k + p for k in near_side] for p in range(PLANE)])
    places = [[k + p for k in far_side] for p in range(PLANE)]
    rest[2:], merged, weight_grad = after(rest[2:], merged, weight_grad)
    merged = merge(w, [rest[0], *rest[2:]], [places[0], *places[2:]], merged)
    last, merged = after(rest[1], merged)
    merged = merge(w, [last], places[1:2], merged)
    return (key_rows, weight_grad, merged, new_anchor, new_momentum)


def solution(mesh):
    split = P("rep", "tp")
    return jax.shard_map(
        body,
        mesh=mesh,
        in_specs=(split, P("tp"), split, split, split, split),
        out_specs=(split,) * 5,
        check_vma=False,
    )
```

```python
import functools
import math

import jax
import jax.numpy as jnp
from jax import lax
from jax.experimental import pallas as pl
from jax.experimental.pallas import tpu as pltpu
from jax.sharding import PartitionSpec as P

HD = 128
PLANE = 4
PAIR = 2 * PLANE
SPAN = 32


momentum_rate = 0.9
outer_rate = 0.7
mix_rate = 0.5
rope_base = 500000.0
norm_eps = 1e-05

VMEM = pl.BlockSpec(memory_space=pltpu.VMEM)
LIGHT = pl.CostEstimate(flops=1, bytes_accessed=1, transcendentals=0)
PARAMS = pltpu.CompilerParams(vmem_limit_bytes=12 * 2**20)


def swap(value, axis, offset):
    size = lax.axis_size(axis)
    if not offset:
        return value
    return lax.ppermute(value, axis, [(i, i ^ offset) for i in range(size)])


def after(*values):
    return lax.optimization_barrier(values)


def rows_at(index, rows):
    return pl.ds(pl.multiple_of(index * rows, rows), rows)


def pick_kernel(groups, w_ref, *out_refs):
    me, core = lax.axis_index("rep"), lax.axis_index("tp")
    rows = out_refs[0].shape[1]
    count = len(groups) * PLANE
    for out, (offsets, p) in zip(out_refs, [(g, p) for g in groups for p in range(PLANE)]):
        for i, k in enumerate(offsets):
            out[i] = w_ref[rows_at(me ^ (k + p), rows), :]
    for k, out in enumerate(out_refs[count:]):
        out[...] = w_ref[rows_at(core ^ k, out.shape[0]), :]


def pick(local_weights, rows, groups):
    cores = lax.axis_size("tp")
    kind = local_weights.dtype
    shapes = [jax.ShapeDtypeStruct((len(g), rows, HD), kind) for g in groups for _ in range(PLANE)]
    shapes += [jax.ShapeDtypeStruct((local_weights.shape[0] // cores, HD), kind)] * cores
    out = pl.pallas_call(
        functools.partial(pick_kernel, groups),
        out_shape=shapes,
        in_specs=[VMEM],
        out_specs=[VMEM] * len(shapes),
        compiler_params=PARAMS,
        cost_estimate=LIGHT,
    )(local_weights)
    count = len(groups) * PLANE
    return [out[i : i + PLANE] for i in range(0, count, PLANE)], out[count:]


def prepare_kernel(grad_ref, cos_ref, sin_ref, out_ref):
    rows = grad_ref.shape[0]
    lane = lax.broadcasted_iota(jnp.int32, (SPAN, HD), 1)
    lower = lane < HD // 2
    pair = jnp.where(lower, lane, lane - HD // 2).astype(jnp.float32)
    freq = jnp.exp(-(pair * 2.0 / HD) * math.log(rope_base))
    step = lax.broadcasted_iota(jnp.int32, (SPAN, HD), 0).astype(jnp.float32)
    near_cos, near_sin = jnp.cos(step * freq), jnp.sin(step * freq)
    near_sin = jnp.where(lower, -near_sin, near_sin)
    for block in range(0, rows // SPAN, SPAN):
        far = (step + block) * SPAN * freq
        far_cos, far_sin = jnp.cos(far), jnp.sin(far)
        far_sin = jnp.where(lower, -far_sin, far_sin)
        for i in range(min(SPAN, rows // SPAN - block)):
            place = pl.ds((block + i) * SPAN, SPAN)
            a_cos, a_sin = far_cos[i : i + 1], far_sin[i : i + 1]
            cosine = a_cos * near_cos - a_sin * near_sin
            signed = a_sin * near_cos + a_cos * near_sin
            cos_ref[place, :] = cosine
            sin_ref[place, :] = signed
            grad = grad_ref[place, :].astype(jnp.float32)
            turned = grad * cosine - pltpu.roll(grad, HD // 2, 1) * signed
            out_ref[place, :] = turned.astype(jnp.bfloat16)


def prepare(key_grad):
    table = jax.ShapeDtypeStruct(key_grad.shape, jnp.float32)
    return pl.pallas_call(
        prepare_kernel,
        out_shape=[table, table, jax.ShapeDtypeStruct(key_grad.shape, jnp.bfloat16)],
        in_specs=[VMEM],
        out_specs=[VMEM] * 3,
        compiler_params=PARAMS,
        cost_estimate=LIGHT,
    )(key_grad)


def squares_kernel(x_ref, out_ref):
    total = None
    for c in range(x_ref.shape[1] // HD):
        x = x_ref[:, c * HD : (c + 1) * HD].astype(jnp.float32)
        total = x * x if total is None else total + x * x
    out_ref[...] = jnp.sum(total.T, axis=0, keepdims=True)


def squares_of(tokens):
    rows, part = tokens.shape
    block = 256
    out = pl.pallas_call(
        squares_kernel,
        out_shape=jax.ShapeDtypeStruct((1, rows), jnp.float32),
        grid=(rows // block,),
        in_specs=[pl.BlockSpec((block, part), lambda i: (i, 0))],
        out_specs=pl.BlockSpec((1, block), lambda i: (0, i)),
        compiler_params=PARAMS,
        cost_estimate=LIGHT,
    )(tokens)
    return out.reshape(rows)


def turn_kernel(inv_width, raw_ref, cos_ref, sin_ref, out_ref):
    keys = raw_ref[...] * inv_width
    turned = keys * cos_ref[...] + pltpu.roll(keys, HD // 2, 1) * sin_ref[...]
    out_ref[...] = turned.astype(jnp.bfloat16)


def turn(inv_width, raw_keys, cosine, signed):
    return pl.pallas_call(
        functools.partial(turn_kernel, inv_width),
        out_shape=jax.ShapeDtypeStruct(raw_keys.shape, jnp.bfloat16),
        in_specs=[VMEM] * 3,
        out_specs=VMEM,
        compiler_params=PARAMS,
        cost_estimate=LIGHT,
    )(raw_keys, cosine, signed)


def normalize(tokens, scale, norm_gain):
    return (tokens.astype(jnp.float32) * scale * norm_gain.astype(jnp.float32)).astype(jnp.bfloat16)


def place_kernel(*refs):
    *block_refs, out_ref = refs
    me = lax.axis_index("tp")
    part = block_refs[0].shape[0]
    for k, block in enumerate(block_refs):
        out_ref[rows_at(me ^ k, part), :] = block[...]


def place_blocks(blocks):
    part, _ = blocks[0].shape
    return pl.pallas_call(
        place_kernel,
        out_shape=jax.ShapeDtypeStruct((len(blocks) * part, HD), blocks[0].dtype),
        in_specs=[VMEM] * len(blocks),
        out_specs=VMEM,
        compiler_params=PARAMS,
        cost_estimate=LIGHT,
    )(*blocks)


def merge_kernel(offsets, w_ref, *refs):
    count = len(offsets)
    out_ref, out_buf, sems = refs[-3:]
    me = lax.axis_index("rep")
    rows = out_buf.shape[1]
    stores = []
    for chunk, ref in zip(offsets, refs):
        for j, k in enumerate(chunk):
            place = rows_at(me ^ k, rows)
            i = len(stores)
            w = w_ref[place, :].astype(jnp.float32)
            g = ref[j].astype(jnp.float32)
            out_buf[i] = (w + mix_rate * (g - w)).astype(jnp.bfloat16)
            stores.append(pltpu.make_async_copy(out_buf.at[i], out_ref.at[place, :], sems.at[i]))
            stores[-1].start()
    for store in stores:
        store.wait()


def merge(local_weights, chunks, offsets, base=None):
    rows = chunks[0].shape[1]
    anywhere = pl.BlockSpec(memory_space=pl.ANY)
    args = [local_weights, *chunks]
    specs = [VMEM] * len(args)
    aliases = {}
    if base is not None:
        aliases = {len(args): 0}
        args.append(base)
        specs.append(anywhere)
    count = sum(map(len, offsets))
    return pl.pallas_call(
        functools.partial(merge_kernel, offsets),
        out_shape=jax.ShapeDtypeStruct(local_weights.shape, jnp.bfloat16),
        in_specs=specs,
        out_specs=anywhere,
        scratch_shapes=[
            pltpu.VMEM((count, rows, HD), jnp.bfloat16),
            pltpu.SemaphoreType.DMA((count,)),
        ],
        input_output_aliases=aliases,
        compiler_params=PARAMS,
        cost_estimate=LIGHT,
    )(*args)


def body(tokens, norm_gain, local_weights, anchor, momentum, key_grad):
    cores = lax.axis_size("tp")
    replicas = lax.axis_size("rep")
    rows, part = tokens.shape
    inv_width = 1.0 / math.sqrt(part * cores)
    far = list(range(PAIR, replicas, PAIR))
    far_side = far + [k + PLANE for k in far]
    near_side = [0, PLANE]
    mates = (1, 2, 3)

    def sum_plane(own, parts):
        total = own.astype(jnp.float32)
        for block in parts:
            total = total + block.astype(jnp.float32)
        return total

    x = [swap(tokens, "tp", k) for k in range(cores)]
    (first, second), halves = pick(local_weights, anchor.shape[0], [far_side, near_side])
    first, second, halves, w, own, key_grad = after(
        first, second, halves, local_weights, tokens, key_grad
    )
    x[0] = own
    first_in = [swap(first[p], "rep", p) for p in mates]
    second_in = [swap(second[p], "rep", p) for p in mates]
    cosine, signed, raw_grad = prepare(key_grad)
    squares = sum(squares_of(block) for block in x)

    first_in, squares, raw_grad, x, norm_gain = after(first_in, squares, raw_grad, x, norm_gain)
    total = sum_plane(first[0], first_in)
    pair = swap(total[len(far) :], "rep", PLANE)
    pair, squares, x, norm_gain = after(pair, squares, x, norm_gain)
    total = total[: len(far)] + pair
    sums = [swap(total[i], "rep", k) for i, k in enumerate(far)]
    gain = [swap(norm_gain, "tp", k) for k in range(cores)]
    scale = lax.rsqrt(squares / (part * cores) + norm_eps)[:, None]

    def key_part(k):
        norm = normalize(x[k], scale, gain[k])
        return jnp.dot(norm, halves[k], preferred_element_type=jnp.float32)

    def weight_rows(k):
        norm = normalize(x[k], scale, gain[k])
        contracted = lax.dot_general(
            norm, raw_grad, (((0,), (0,)), ((), ())), preferred_element_type=jnp.float32
        )
        return (contracted * inv_width).astype(jnp.bfloat16)

    raw_keys = sum(key_part(k) for k in range(cores))

    second_in, raw_keys, x = after(second_in, raw_keys, x)
    total = sum_plane(second[0], second_in)
    sums.append(swap(total[1], "rep", PLANE))

    key_rows = turn(inv_width, raw_keys, cosine, signed)
    sums[: len(far)], x, scale = after(sums[: len(far)], x, scale)
    blocks = [weight_rows(0)]
    sums, key_rows, blocks, x, scale, gain = after(sums, key_rows, blocks, x, scale, gain)

    def update(parts, anchor, momentum):
        change = anchor - sum(parts) / replicas
        new_momentum = momentum_rate * momentum + change
        new_anchor = anchor - outer_rate * (change + momentum_rate * new_momentum)
        return new_anchor, new_momentum

    parts = [total[0], *sums]
    outgoing = update(parts, anchor, momentum)[0].astype(jnp.bfloat16)[None]

    mate = swap(outgoing, "rep", PLANE)
    column = [swap(outgoing, "rep", k) for k in far_side]
    mate, x, parts, anchor, momentum = after(mate, x, parts, anchor, momentum)
    near = jnp.concatenate([outgoing, mate])
    near = [near] + [swap(near, "rep", p) for p in mates]
    blocks += [weight_rows(k) for k in range(1, cores)]
    column, blocks = after(column, blocks)
    rest = jnp.concatenate(column)
    rest = [rest] + [swap(rest, "rep", p) for p in mates]
    weight_grad = place_blocks(blocks)
    outer = update(parts, anchor, momentum)
    near, weight_grad, (new_anchor, new_momentum) = after(near, weight_grad, outer)
    merged = merge(w, near, [[k + p for k in near_side] for p in range(PLANE)])
    places = [[k + p for k in far_side] for p in range(PLANE)]
    weight_grad, merged, *rest = after(weight_grad, merged, *rest)
    merged = merge(w, rest, places, merged)
    return (key_rows, weight_grad, merged, new_anchor, new_momentum)


def solution(mesh):
    split = P("rep", "tp")
    return jax.shard_map(
        body,
        mesh=mesh,
        in_specs=(split, P("tp"), split, split, split, split),
        out_specs=(split,) * 5,
        check_vma=False,
    )
```

```python
import functools
import math

import jax
import jax.numpy as jnp
from jax import lax
from jax.experimental import pallas as pl
from jax.experimental.pallas import tpu as pltpu
from jax.sharding import PartitionSpec as P

HD = 128
PLANE = 4
PAIR = 2 * PLANE
SPAN = 32


momentum_rate = 0.9
outer_rate = 0.7
mix_rate = 0.5
rope_base = 500000.0
norm_eps = 1e-05

VMEM = pl.BlockSpec(memory_space=pltpu.VMEM)
LIGHT = pl.CostEstimate(flops=1, bytes_accessed=1, transcendentals=0)
PARAMS = pltpu.CompilerParams(vmem_limit_bytes=12 * 2**20)


def swap(value, axis, offset):
    size = lax.axis_size(axis)
    if not offset:
        return value
    return lax.ppermute(value, axis, [(i, i ^ offset) for i in range(size)])


def after(*values):
    return lax.optimization_barrier(values)


def rows_at(index, rows):
    return pl.ds(pl.multiple_of(index * rows, rows), rows)


def pick_kernel(groups, w_ref, *out_refs):
    me, core = lax.axis_index("rep"), lax.axis_index("tp")
    rows = out_refs[0].shape[1]
    count = len(groups) * PLANE
    for out, (offsets, p) in zip(out_refs, [(g, p) for g in groups for p in range(PLANE)]):
        for i, k in enumerate(offsets):
            out[i] = w_ref[rows_at(me ^ (k + p), rows), :]
    for k, out in enumerate(out_refs[count:]):
        out[...] = w_ref[rows_at(core ^ k, out.shape[0]), :]


def pick(local_weights, rows, groups):
    cores = lax.axis_size("tp")
    kind = local_weights.dtype
    shapes = [jax.ShapeDtypeStruct((len(g), rows, HD), kind) for g in groups for _ in range(PLANE)]
    shapes += [jax.ShapeDtypeStruct((local_weights.shape[0] // cores, HD), kind)] * cores
    out = pl.pallas_call(
        functools.partial(pick_kernel, groups),
        out_shape=shapes,
        in_specs=[VMEM],
        out_specs=[VMEM] * len(shapes),
        compiler_params=PARAMS,
        cost_estimate=LIGHT,
    )(local_weights)
    count = len(groups) * PLANE
    return [out[i : i + PLANE] for i in range(0, count, PLANE)], out[count:]


def prepare_kernel(grad_ref, cos_ref, sin_ref, out_ref):
    rows = grad_ref.shape[0]
    lane = lax.broadcasted_iota(jnp.int32, (SPAN, HD), 1)
    lower = lane < HD // 2
    pair = jnp.where(lower, lane, lane - HD // 2).astype(jnp.float32)
    freq = jnp.exp(-(pair * 2.0 / HD) * math.log(rope_base))
    step = lax.broadcasted_iota(jnp.int32, (SPAN, HD), 0).astype(jnp.float32)
    near_cos, near_sin = jnp.cos(step * freq), jnp.sin(step * freq)
    near_sin = jnp.where(lower, -near_sin, near_sin)
    for block in range(0, rows // SPAN, SPAN):
        far = (step + block) * SPAN * freq
        far_cos, far_sin = jnp.cos(far), jnp.sin(far)
        far_sin = jnp.where(lower, -far_sin, far_sin)
        for i in range(min(SPAN, rows // SPAN - block)):
            place = pl.ds((block + i) * SPAN, SPAN)
            a_cos, a_sin = far_cos[i : i + 1], far_sin[i : i + 1]
            cosine = a_cos * near_cos - a_sin * near_sin
            signed = a_sin * near_cos + a_cos * near_sin
            cos_ref[place, :] = cosine
            sin_ref[place, :] = signed
            grad = grad_ref[place, :].astype(jnp.float32)
            turned = grad * cosine - pltpu.roll(grad, HD // 2, 1) * signed
            out_ref[place, :] = turned.astype(jnp.bfloat16)


def prepare(key_grad):
    table = jax.ShapeDtypeStruct(key_grad.shape, jnp.float32)
    return pl.pallas_call(
        prepare_kernel,
        out_shape=[table, table, jax.ShapeDtypeStruct(key_grad.shape, jnp.bfloat16)],
        in_specs=[VMEM],
        out_specs=[VMEM] * 3,
        compiler_params=PARAMS,
        cost_estimate=LIGHT,
    )(key_grad)


def squares_kernel(x_ref, out_ref):
    total = None
    for c in range(x_ref.shape[1] // HD):
        x = x_ref[:, c * HD : (c + 1) * HD].astype(jnp.float32)
        total = x * x if total is None else total + x * x
    out_ref[...] = jnp.sum(total.T, axis=0, keepdims=True)


def squares_of(tokens):
    rows, part = tokens.shape
    block = 256
    out = pl.pallas_call(
        squares_kernel,
        out_shape=jax.ShapeDtypeStruct((1, rows), jnp.float32),
        grid=(rows // block,),
        in_specs=[pl.BlockSpec((block, part), lambda i: (i, 0))],
        out_specs=pl.BlockSpec((1, block), lambda i: (0, i)),
        compiler_params=PARAMS,
        cost_estimate=LIGHT,
    )(tokens)
    return out.reshape(rows)


def turn_kernel(inv_width, raw_ref, cos_ref, sin_ref, out_ref):
    keys = raw_ref[...] * inv_width
    turned = keys * cos_ref[...] + pltpu.roll(keys, HD // 2, 1) * sin_ref[...]
    out_ref[...] = turned.astype(jnp.bfloat16)


def turn(inv_width, raw_keys, cosine, signed):
    return pl.pallas_call(
        functools.partial(turn_kernel, inv_width),
        out_shape=jax.ShapeDtypeStruct(raw_keys.shape, jnp.bfloat16),
        in_specs=[VMEM] * 3,
        out_specs=VMEM,
        compiler_params=PARAMS,
        cost_estimate=LIGHT,
    )(raw_keys, cosine, signed)


def normalize(tokens, scale, norm_gain):
    return (tokens.astype(jnp.float32) * scale * norm_gain.astype(jnp.float32)).astype(jnp.bfloat16)


def place_kernel(*refs):
    *block_refs, out_ref = refs
    me = lax.axis_index("tp")
    part = block_refs[0].shape[0]
    for k, block in enumerate(block_refs):
        out_ref[rows_at(me ^ k, part), :] = block[...]


def place_blocks(blocks):
    part, _ = blocks[0].shape
    return pl.pallas_call(
        place_kernel,
        out_shape=jax.ShapeDtypeStruct((len(blocks) * part, HD), blocks[0].dtype),
        in_specs=[VMEM] * len(blocks),
        out_specs=VMEM,
        compiler_params=PARAMS,
        cost_estimate=LIGHT,
    )(*blocks)


def merge_kernel(offsets, w_ref, *refs):
    count = len(offsets)
    out_ref, out_buf, sems = refs[-3:]
    me = lax.axis_index("rep")
    rows = out_buf.shape[1]
    stores = []
    for chunk, ref in zip(offsets, refs):
        for j, k in enumerate(chunk):
            place = rows_at(me ^ k, rows)
            i = len(stores)
            w = w_ref[place, :].astype(jnp.float32)
            g = ref[j].astype(jnp.float32)
            out_buf[i] = (w + mix_rate * (g - w)).astype(jnp.bfloat16)
            stores.append(pltpu.make_async_copy(out_buf.at[i], out_ref.at[place, :], sems.at[i]))
            stores[-1].start()
    for store in stores:
        store.wait()


def merge(local_weights, chunks, offsets, base=None):
    rows = chunks[0].shape[1]
    anywhere = pl.BlockSpec(memory_space=pl.ANY)
    args = [local_weights, *chunks]
    specs = [VMEM] * len(args)
    aliases = {}
    if base is not None:
        aliases = {len(args): 0}
        args.append(base)
        specs.append(anywhere)
    count = sum(map(len, offsets))
    return pl.pallas_call(
        functools.partial(merge_kernel, offsets),
        out_shape=jax.ShapeDtypeStruct(local_weights.shape, jnp.bfloat16),
        in_specs=specs,
        out_specs=anywhere,
        scratch_shapes=[
            pltpu.VMEM((count, rows, HD), jnp.bfloat16),
            pltpu.SemaphoreType.DMA((count,)),
        ],
        input_output_aliases=aliases,
        compiler_params=PARAMS,
        cost_estimate=LIGHT,
    )(*args)


def body(tokens, norm_gain, local_weights, anchor, momentum, key_grad):
    cores = lax.axis_size("tp")
    replicas = lax.axis_size("rep")
    rows, part = tokens.shape
    inv_width = 1.0 / math.sqrt(part * cores)
    far = list(range(PAIR, replicas, PAIR))
    far_side = far + [k + PLANE for k in far]
    near_side = [0, PLANE]
    mates = (1, 2, 3)

    def sum_plane(own, parts):
        total = own.astype(jnp.float32)
        for block in parts:
            total = total + block.astype(jnp.float32)
        return total

    x = [swap(tokens, "tp", k) for k in range(cores)]
    (first, second), halves = pick(local_weights, anchor.shape[0], [far_side, near_side])
    first, second, halves, w, own, key_grad = after(
        first, second, halves, local_weights, tokens, key_grad
    )
    x[0] = own
    first_in = [swap(first[p], "rep", p) for p in reversed(mates)]
    second_in = [swap(second[p], "rep", p) for p in reversed(mates)]
    cosine, signed, raw_grad = prepare(key_grad)
    squares = sum(squares_of(block) for block in x)

    first_in, squares, raw_grad, x, norm_gain = after(first_in, squares, raw_grad, x, norm_gain)
    total = sum_plane(first[0], first_in)
    pair = swap(total[len(far) :], "rep", PLANE)
    pair, squares, x, norm_gain = after(pair, squares, x, norm_gain)
    total = total[: len(far)] + pair
    sums = [swap(total[i], "rep", k) for i, k in enumerate(far)]
    gain = [swap(norm_gain, "tp", k) for k in range(cores)]
    scale = lax.rsqrt(squares / (part * cores) + norm_eps)[:, None]

    def key_part(k):
        norm = normalize(x[k], scale, gain[k])
        return jnp.dot(norm, halves[k], preferred_element_type=jnp.float32)

    def weight_rows(k):
        norm = normalize(x[k], scale, gain[k])
        contracted = lax.dot_general(
            norm, raw_grad, (((0,), (0,)), ((), ())), preferred_element_type=jnp.float32
        )
        return (contracted * inv_width).astype(jnp.bfloat16)

    raw_keys = sum(key_part(k) for k in range(cores))

    second_in, raw_keys, x = after(second_in, raw_keys, x)
    total = sum_plane(second[0], second_in)
    sums.append(swap(total[1], "rep", PLANE))

    key_rows = turn(inv_width, raw_keys, cosine, signed)
    sums[: len(far)], x, scale = after(sums[: len(far)], x, scale)
    blocks = [weight_rows(0)]
    sums, key_rows, blocks, x, scale, gain = after(sums, key_rows, blocks, x, scale, gain)

    def update(parts, anchor, momentum):
        change = anchor - sum(parts) / replicas
        new_momentum = momentum_rate * momentum + change
        new_anchor = anchor - outer_rate * (change + momentum_rate * new_momentum)
        return new_anchor, new_momentum

    parts = [total[0], *sums]
    outgoing = update(parts, anchor, momentum)[0].astype(jnp.bfloat16)[None]

    mate = swap(outgoing, "rep", PLANE)
    column = [swap(outgoing, "rep", k) for k in far_side]
    mate, x, parts, anchor, momentum = after(mate, x, parts, anchor, momentum)
    near = jnp.concatenate([outgoing, mate])
    near = [near] + [swap(near, "rep", p) for p in mates]
    blocks += [weight_rows(k) for k in range(1, cores)]
    column, blocks = after(column, blocks)
    rest = jnp.concatenate(column)
    rest = [rest] + [swap(rest, "rep", p) for p in mates]
    weight_grad = place_blocks(blocks)
    outer = update(parts, anchor, momentum)
    near, weight_grad, (new_anchor, new_momentum) = after(near, weight_grad, outer)
    merged = merge(w, near, [[k + p for k in near_side] for p in range(PLANE)])
    places = [[k + p for k in far_side] for p in range(PLANE)]
    weight_grad, merged, *rest = after(weight_grad, merged, *rest)
    merged = merge(w, rest, places, merged)
    return (key_rows, weight_grad, merged, new_anchor, new_momentum)


def solution(mesh):
    split = P("rep", "tp")
    return jax.shard_map(
        body,
        mesh=mesh,
        in_specs=(split, P("tp"), split, split, split, split),
        out_specs=(split,) * 5,
        check_vma=False,
    )
```
